512 devices in a mesh: group: 16 (over y, x), dev: 32 (over z, core).
Axes of the slice: x: 4, y: 4, z: 16, core: 2. Of those that a mesh axis runs over, the one named last changes fastest.
Arguments:
- embeddings: float32 [262144, 768], P(('group', 'dev'))
- owner: int32 [262144], P(('group', 'dev')), may hold values from 0 to 31, as said below
Outputs:
- self_max: float32 [262144], P(('group', 'dev'))
- next_max: float32 [262144], P(('group', 'dev'))
- prev_max: float32 [262144], P(('group', 'dev'))
The draws below stay inside these ranges and needn't reach their ends.
Inputs may be any that keep to these rules, and one draw needn't show every extreme that they name: `owner`: no device sends more than 32 of its vectors to one cluster; in each group one cluster takes exactly 32 vectors from every device of the group.
All inputs are finite; a program needn't handle non-finite values.
Results may differ from the reference program's by a relative error of at most 0.0004.
Values may be sent and summed in bfloat16 or wider, within the bound.
A program may use at most 64 MiB of HBM per device.

```python
import jax
import jax.numpy as jnp
from jax import lax

D = 768
ROWS_DEV = 512
OWNERS = 32
GROUPS = 16
CAP = 32
VEC = 262144


def owner_table(key):

    def one_group(group_key):
        fullest = jax.random.randint(jax.random.fold_in(group_key, 1), (), 0, OWNERS).astype(jnp.int32)

        def one_source(source_key):
            others = (fullest + 1 + jnp.arange((OWNERS - 1) * CAP, dtype=jnp.int32) // CAP) % OWNERS
            picked = jax.random.permutation(jax.random.fold_in(source_key, 2), others)[:ROWS_DEV - CAP]
            listed = jnp.concatenate([jnp.full((CAP,), fullest, jnp.int32), picked.astype(jnp.int32)])
            return jax.random.permutation(jax.random.fold_in(source_key, 3), listed)
        source_keys = jax.random.split(jax.random.fold_in(group_key, 4), OWNERS)
        return jax.vmap(one_source)(source_keys)
    group_keys = jax.random.split(jax.random.fold_in(key, 77), GROUPS)
    return jax.vmap(one_group)(group_keys).reshape(VEC).astype(jnp.int32)


def draw_owner(key, part):
    return owner_table(key)


def draw_embeddings(key, part):
    ids = owner_table(key).reshape(GROUPS, OWNERS * ROWS_DEV)
    base = jax.random.normal(jax.random.fold_in(key, 11), (OWNERS, D), jnp.float32)
    moved = jax.random.normal(jax.random.fold_in(key, 12), (GROUPS, OWNERS, D), jnp.float32)
    centre = base[None, :, :] + 0.8 * moved
    group_index = jnp.arange(GROUPS, dtype=jnp.int32)[:, None]
    row_centre = centre[group_index, ids]
    spread = jnp.exp(jax.random.uniform(jax.random.fold_in(key, 13), (GROUPS, OWNERS * ROWS_DEV, 1), jnp.float32, jnp.log(0.6), jnp.log(2.5)))
    flip_draw = jax.random.uniform(jax.random.fold_in(key, 16), (GROUPS, OWNERS * ROWS_DEV, 1), jnp.float32)
    facing = jnp.where(flip_draw < 1.0 / ROWS_DEV, -1.0, 1.0).astype(jnp.float32)
    noise = jax.random.normal(jax.random.fold_in(key, 14), (GROUPS, OWNERS * ROWS_DEV, D), jnp.float32)
    values = facing * row_centre + spread * noise
    return values.reshape(VEC, D).astype(jnp.float32)


def setup_inputs(seed: int = 0) -> dict:
    keys = jax.random.split(jax.random.key(seed), 3)
    return {
        "embeddings": draw_embeddings(jax.random.fold_in(keys[2], 71), 0),
        "owner": draw_owner(jax.random.fold_in(keys[2], 71), 0),
    }


def unit_rows(embeddings):
    norm = lax.optimization_barrier(jnp.sum(embeddings * embeddings, axis=-1, keepdims=True))
    return (embeddings * lax.rsqrt(norm + 1e-06)).astype(jnp.bfloat16)

def slot_ranks(owner_rows):
    onehot = (owner_rows[:, None] == jnp.arange(OWNERS, dtype=jnp.int32)[None, :]).astype(jnp.int32)
    before = jnp.cumsum(onehot, axis=0) - onehot
    return lax.optimization_barrier(jnp.sum(before * onehot, axis=1)).astype(jnp.int32)

def pack_group(unit_group, owner_group):
    ranks = jax.vmap(slot_ranks)(owner_group)
    column = (jnp.arange(OWNERS, dtype=jnp.int32)[:, None] * CAP + ranks).astype(jnp.int32)
    slots = jnp.zeros((OWNERS, OWNERS * CAP, D), jnp.bfloat16).at[owner_group, column].set(unit_group)
    live = jnp.zeros((OWNERS, OWNERS * CAP), jnp.int32).at[owner_group, column].set(1)
    return (slots, live, column)

def best_match(left, right, live_right, skip_self):
    scores = jnp.dot(left, right.T, preferred_element_type=jnp.float32)
    keep = live_right[None, :] > 0
    if skip_self:
        size = left.shape[0]
        same = lax.broadcasted_iota(jnp.int32, (size, size), 0) == lax.broadcasted_iota(jnp.int32, (size, size), 1)
        keep = keep & jnp.logical_not(same)
    return lax.optimization_barrier(jnp.max(jnp.where(keep, scores, -1.0), axis=1))

def reference(embeddings, owner):
    unit = unit_rows(embeddings).reshape(GROUPS, OWNERS, ROWS_DEV, D)
    owner_ids = owner.reshape(GROUPS, OWNERS, ROWS_DEV)

    def per_group(group):
        later = (group + 1) % GROUPS
        earlier = (group + GROUPS - 1) % GROUPS
        slots, live, column = pack_group(unit[group], owner_ids[group])
        next_slots, next_live, unused_one = pack_group(unit[later], owner_ids[later])
        prev_slots, prev_live, unused_two = pack_group(unit[earlier], owner_ids[earlier])

        def per_cluster(cluster):
            own = slots[cluster]
            return (best_match(own, own, live[cluster], True), best_match(own, next_slots[cluster], next_live[cluster], False), best_match(own, prev_slots[cluster], prev_live[cluster], False))
        self_slot, next_slot, prev_slot = lax.map(per_cluster, jnp.arange(OWNERS, dtype=jnp.int32))
        mine = owner_ids[group]
        return (self_slot[mine, column], next_slot[mine, column], prev_slot[mine, column])
    self_all, next_all, prev_all = lax.map(per_group, jnp.arange(GROUPS, dtype=jnp.int32))
    return (self_all.reshape(VEC), next_all.reshape(VEC), prev_all.reshape(VEC))
```

```python
import functools

import jax
import jax.numpy as jnp
from jax import lax
from jax.experimental import pallas as pl
from jax.experimental.pallas import tpu as pltpu
from jax.sharding import PartitionSpec as P

CAP = 32
DEAD = 2.0
STAGE = 8
PIECE = 4
MESH = pl.DeviceIdType.MESH


def ring_offset(k, nz):
    j = k // 2
    size = nz // 2 - (j + 1) // 2
    return jnp.where(j % 2 == 1, size, -size)


def kernel(
    emb_hbm,
    owner_ref,
    self_ref,
    next_ref,
    prev_ref,
    emb,
    unit,
    outgoing,
    own,
    before,
    after,
    acc,
    ret,
    got,
    load_sem,
    send_sem,
    recv_sem,
    pair_send,
    pair_recv,
    ret_send,
    ret_recv,
    *,
    groups,
    owners,
):
    rows, width = emb.shape
    nz = owners // 2
    group = lax.axis_index("group")
    me = lax.axis_index("dev")
    mez, mec = me // 2, me % 2
    stages = owners // STAGE
    here = owners - 2

    load = pltpu.make_async_copy(emb_hbm, emb, load_sem)
    load.start()

    def target(k):
        z = (mez + ring_offset(k, nz) + nz) % nz
        return 2 * z + (mec + k) % 2

    def source(k):
        z = (mez - ring_offset(k, nz) + nz) % nz
        return 2 * z + (mec + k) % 2

    barrier = pltpu.get_barrier_semaphore()

    def greet(d, carry):
        pl.semaphore_signal(barrier, inc=1, device_id={"dev": (me + d) % owners}, device_id_type=MESH)
        return carry

    lax.fori_loop(1, owners, greet, 0)
    later = (group + 1) % groups
    earlier = (group + groups - 1) % groups
    pl.semaphore_signal(barrier, inc=1, device_id={"group": later}, device_id_type=MESH)
    pl.semaphore_signal(barrier, inc=1, device_id={"group": earlier}, device_id_type=MESH)

    owner = jnp.concatenate([owner_ref[a : a + 1, :] for a in range(rows // 128)], axis=1)
    chunk = lax.broadcasted_iota(jnp.int32, (owners, 1), 0)
    cluster = 2 * ((mez + ring_offset(chunk, nz) + nz) % nz) + (mec + chunk) % 2
    hot = owner == cluster
    hot_f = jnp.where(hot, 1.0, 0.0)
    hot_b = hot_f.astype(jnp.bfloat16)
    earlier_row = lax.broadcasted_iota(jnp.int32, (rows, rows), 0) < lax.broadcasted_iota(
        jnp.int32, (rows, rows), 1
    )
    ahead = jnp.dot(
        hot_b, jnp.where(earlier_row, 1.0, 0.0).astype(jnp.bfloat16), preferred_element_type=jnp.float32
    )
    rank = jnp.sum(ahead * hot_f, axis=0, keepdims=True).astype(jnp.int32)
    chunk_of = jnp.sum(hot_f * chunk.astype(jnp.float32), axis=0, keepdims=True).astype(jnp.int32)
    slot_of = chunk_of * CAP + rank
    count = jnp.sum(hot_f, axis=1, keepdims=True)

    load.wait()
    raw = emb[...]
    norm = jnp.sum(raw * raw, axis=-1, keepdims=True)
    unit[...] = (raw * lax.rsqrt(norm + 1e-06)).astype(jnp.bfloat16)

    def dispatch(k):
        return pltpu.make_async_remote_copy(
            src_ref=outgoing.at[k],
            dst_ref=own.at[k],
            send_sem=send_sem.at[k],
            recv_sem=recv_sem.at[k],
            device_id={"dev": target(k)},
            device_id_type=MESH,
        )

    def start_dispatch(k, carry):
        dispatch(k).start()
        return carry

    slot = lax.broadcasted_iota(jnp.int32, (STAGE * CAP, 1), 0)
    first = lax.broadcasted_iota(jnp.int32, (CAP, width), 1) == 0
    in_chunk = lax.broadcasted_iota(jnp.int32, (CAP, width), 0).astype(jnp.float32)
    for t in range(stages):
        pick = jnp.where(slot_of == slot + t * STAGE * CAP, 1.0, 0.0).astype(jnp.bfloat16)
        packed = jnp.dot(pick, unit[...], preferred_element_type=jnp.float32)
        for c in range(STAGE):
            k = t * STAGE + c
            empty = first & (in_chunk >= count[k : k + 1, :])
            piece = jnp.where(empty, DEAD, packed[c * CAP : (c + 1) * CAP, :]).astype(jnp.bfloat16)
            if k == here:
                own[k] = piece
            else:
                outgoing[k] = piece
        if t == 0:
            pl.semaphore_wait(barrier, owners + 1)
        if t < stages - 1:
            lax.fori_loop(t * STAGE, (t + 1) * STAGE, start_dispatch, 0)
        else:
            lax.fori_loop(t * STAGE, here, start_dispatch, 0)
            dispatch(owners - 1).start()

    acc[...] = jnp.full_like(acc, -4.0)

    def forward(p, way):
        part = pl.ds(p * PIECE, PIECE)
        return pltpu.make_async_remote_copy(
            src_ref=own.at[part],
            dst_ref=(before if way == 0 else after).at[part],
            send_sem=pair_send.at[way, p],
            recv_sem=pair_recv.at[way, p],
            device_id={"group": later if way == 0 else earlier},
            device_id_type=MESH,
        )

    def block(which, found, jb, ib, diagonal=False):
        right = found[pl.ds(jb * STAGE, STAGE)].reshape(STAGE * CAP, width)
        left = own[pl.ds(ib * STAGE, STAGE)].reshape(STAGE * CAP, width)
        scores = lax.dot_general(right, left, (((1,), (1,)), ((), ())), preferred_element_type=jnp.float32)
        drop = right[:, :128].astype(jnp.float32)[:, 0:1] > 1.5
        if diagonal:
            size = STAGE * CAP
            drop = drop | (
                lax.broadcasted_iota(jnp.int32, (size, size), 0) == lax.broadcasted_iota(jnp.int32, (size, size), 1)
            )
        scores = jnp.where(drop, -1.0, scores)
        best = jnp.max(scores.reshape(STAGE * CAP // 8, 8, STAGE * CAP), axis=0)
        acc[which, ib] = jnp.maximum(acc[which, ib], best)

    def arrive(t):
        def chunk_arrives(k, carry):
            dispatch(k).wait_recv()
            return carry

        def piece_arrives(p, carry):
            lax.fori_loop(p * PIECE, (p + 1) * PIECE, chunk_arrives, 0)
            forward(p, 0).start()
            forward(p, 1).start()
            return carry

        per = STAGE // PIECE
        if t < stages - 1:
            lax.fori_loop(t * per, (t + 1) * per, piece_arrives, 0)
        else:
            lax.fori_loop(t * per, (t + 1) * per - 1, piece_arrives, 0)
            lax.fori_loop(owners - PIECE, here, chunk_arrives, 0)
            dispatch(owners - 1).wait_recv()
            forward((t + 1) * per - 1, 0).start()
            forward((t + 1) * per - 1, 1).start()

    def pair_arrives(t):
        def piece(p, carry):
            forward(p, 0).wait_recv()
            forward(p, 1).wait_recv()
            return carry

        per = STAGE // PIECE
        lax.fori_loop(t * per, (t + 1) * per, piece, 0)

    def both(jb, ib):
        block(1, after, jb, ib)
        block(2, before, jb, ib)

    for t in range(stages):
        arrive(t)
        block(0, own, t, t, diagonal=True)

        def own_blocks(b, carry, t=t):
            block(0, own, t, b)
            block(0, own, b, t)
            return carry

        lax.fori_loop(0, t, own_blocks, 0)
        if t > 0:
            pair_arrives(t - 1)

            def new_rows(b, carry, t=t):
                both(b, t)
                return carry

            def new_found(b, carry, t=t):
                both(t - 1, b)
                return carry

            lax.fori_loop(0, t, new_rows, 0)
            lax.fori_loop(0, t, new_found, 0)
    pair_arrives(stages - 1)

    def last_found(b, carry):
        both(stages - 1, b)
        return carry

    lax.fori_loop(0, stages, last_found, 0)

    tiles = []
    for which in range(3):
        parts = []
        for b in range(stages):
            best = jnp.max(acc[which, b], axis=0, keepdims=True)
            parts += [best[:, h * 128 : (h + 1) * 128] for h in range(STAGE * CAP // 128)]
        tiles.append(jnp.concatenate(parts, axis=0))
    lane = lax.broadcasted_iota(jnp.int32, tiles[0].shape, 1)
    per_tile = 128 // CAP
    for j in range(per_tile):
        moved = [pltpu.roll(tiles[w], (CAP * (w - j)) % 128, 1) if (w - j) % 4 else tiles[w] for w in range(3)]
        mixed = jnp.where(lane < CAP, moved[0], jnp.where(lane < 2 * CAP, moved[1], moved[2]))
        for t in range(owners // per_tile):
            k = per_tile * t + j
            if k == here:
                got[k] = mixed[t : t + 1, :]
            else:
                ret[k] = mixed[t : t + 1, :]

    def give_back(k):
        return pltpu.make_async_remote_copy(
            src_ref=ret.at[k],
            dst_ref=got.at[k],
            send_sem=ret_send.at[k],
            recv_sem=ret_recv.at[k],
            device_id={"dev": source(k)},
            device_id_type=MESH,
        )

    def start_back(k, carry):
        give_back(k).start()
        return carry

    lax.fori_loop(0, here, start_back, 0)
    give_back(owners - 1).start()

    def drain(k, carry):
        dispatch(k).wait_send()
        return carry

    lax.fori_loop(0, here, drain, 0)
    dispatch(owners - 1).wait_send()

    def drain_pair(p, carry):
        forward(p, 0).wait_send()
        forward(p, 1).wait_send()
        return carry

    lax.fori_loop(0, owners // PIECE, drain_pair, 0)

    def wait_back(k, carry):
        give_back(k).wait()
        return carry

    lax.fori_loop(0, here, wait_back, 0)
    give_back(owners - 1).wait()

    table = got[...].reshape(owners, 128)
    high = table.astype(jnp.bfloat16)
    rest = table - high.astype(jnp.float32)
    middle = rest.astype(jnp.bfloat16)
    low = (rest - middle.astype(jnp.float32)).astype(jnp.bfloat16)
    stacked = jnp.concatenate([high, middle, low], axis=0)
    picks = jnp.concatenate([hot_b, hot_b, hot_b], axis=0)
    found = lax.dot_general(stacked, picks, (((0,), (0,)), ((), ())), preferred_element_type=jnp.float32)
    mine = lax.broadcasted_iota(jnp.int32, (CAP, 1), 0) == rank
    for which, ref in enumerate((self_ref, next_ref, prev_ref)):
        kept = jnp.where(mine, found[which * CAP : (which + 1) * CAP, :], 0.0)
        line = jnp.sum(kept, axis=0, keepdims=True)
        for a in range(rows // 128):
            ref[a : a + 1, :] = line[:, a * 128 : (a + 1) * 128]


def local(embeddings, owner):
    owners = lax.axis_size("dev")
    groups = lax.axis_size("group")
    rows, width = embeddings.shape
    vmem = pl.BlockSpec(memory_space=pltpu.VMEM)
    slots = (owners, CAP, width)
    result = jax.ShapeDtypeStruct((rows // 128, 128), jnp.float32)
    outs = pl.pallas_call(
        functools.partial(kernel, groups=groups, owners=owners),
        out_shape=(result, result, result),
        in_specs=[pl.BlockSpec(memory_space=pl.ANY), vmem],
        out_specs=(vmem, vmem, vmem),
        scratch_shapes=[
            pltpu.VMEM((rows, width), jnp.float32),
            pltpu.VMEM((rows, width), jnp.bfloat16),
            pltpu.VMEM(slots, jnp.bfloat16),
            pltpu.VMEM(slots, jnp.bfloat16),
            pltpu.VMEM(slots, jnp.bfloat16),
            pltpu.VMEM(slots, jnp.bfloat16),
            pltpu.VMEM((3, owners // STAGE, 8, STAGE * CAP), jnp.float32),
            pltpu.VMEM((owners, 1, 128), jnp.float32),
            pltpu.VMEM((owners, 1, 128), jnp.float32),
            pltpu.SemaphoreType.DMA,
            pltpu.SemaphoreType.DMA((owners,)),
            pltpu.SemaphoreType.DMA((owners,)),
            pltpu.SemaphoreType.DMA((2, owners // PIECE)),
            pltpu.SemaphoreType.DMA((2, owners // PIECE)),
            pltpu.SemaphoreType.DMA((owners,)),
            pltpu.SemaphoreType.DMA((owners,)),
        ],
        compiler_params=pltpu.CompilerParams(
            collective_id=0, has_side_effects=True, vmem_limit_bytes=40 * 1024 * 1024
        ),
    )(embeddings, owner.reshape(rows // 128, 128))
    return tuple(o.reshape(rows) for o in outs)


def solution(mesh):
    placed = (P(("group", "dev"), None), P(("group", "dev")))
    return jax.shard_map(
        local,
        mesh=mesh,
        in_specs=placed,
        out_specs=(P(("group", "dev")), P(("group", "dev")), P(("group", "dev"))),
        check_vma=False,
    )
```

```python
import functools

import jax
import jax.numpy as jnp
from jax import lax
from jax.experimental import pallas as pl
from jax.experimental.pallas import tpu as pltpu
from jax.sharding import PartitionSpec as P

CAP = 32
DEAD = 2.0
STAGE = 8
PIECE = 1
PACK = 4
RELAYED = (2, 3)
MESH = pl.DeviceIdType.MESH


def ring_offset(k, nz):
    j = k // 2
    size = jnp.where(j == 0, 0, nz // 2 - j // 2)
    return jnp.where(j % 2 == 0, size, -size)


def kernel(
    emb_hbm,
    owner_hbm,
    out_ref,
    emb,
    owner_ref,
    unit,
    outgoing,
    own,
    before,
    after,
    acc,
    ret,
    got,
    relay,
    load_sem,
    send_sem,
    recv_sem,
    pair_send,
    pair_recv,
    ret_send,
    ret_recv,
    relay_send,
    relay_recv,
    *,
    groups,
    owners,
):
    rows, width = emb.shape
    nz = owners // 2
    group = lax.axis_index("group")
    me = lax.axis_index("dev")
    mez, mec = me // 2, me % 2
    stages = owners // STAGE
    here = 0

    load_owner = pltpu.make_async_copy(owner_hbm, owner_ref, load_sem.at[0])
    load_owner.start()
    load = pltpu.make_async_copy(emb_hbm, emb, load_sem.at[1])
    load.start()

    def target(k):
        z = (mez + ring_offset(k, nz) + nz) % nz
        return 2 * z + (mec + k) % 2

    def source(k):
        z = (mez - ring_offset(k, nz) + nz) % nz
        return 2 * z + (mec + k) % 2

    barrier = pltpu.get_barrier_semaphore()

    def greet(d, carry):
        pl.semaphore_signal(barrier, inc=1, device_id={"dev": (me + d) % owners}, device_id_type=MESH)
        return carry

    lax.fori_loop(1, owners, greet, 0)
    later = (group + 1) % groups
    earlier = (group + groups - 1) % groups
    pl.semaphore_signal(barrier, inc=1, device_id={"group": later}, device_id_type=MESH)
    pl.semaphore_signal(barrier, inc=1, device_id={"group": earlier}, device_id_type=MESH)

    load_owner.wait()

    owner = jnp.concatenate([owner_ref[a : a + 1, :] for a in range(rows // 128)], axis=1)
    chunk = lax.broadcasted_iota(jnp.int32, (owners, 1), 0)
    cluster = 2 * ((mez + ring_offset(chunk, nz) + nz) % nz) + (mec + chunk) % 2
    hot = owner == cluster
    hot_f = jnp.where(hot, 1.0, 0.0)
    hot_b = hot_f.astype(jnp.bfloat16)
    earlier_row = lax.broadcasted_iota(jnp.int32, (rows, rows), 0) < lax.broadcasted_iota(
        jnp.int32, (rows, rows), 1
    )
    ahead = jnp.dot(
        hot_b, jnp.where(earlier_row, 1.0, 0.0).astype(jnp.bfloat16), preferred_element_type=jnp.float32
    )
    rank = jnp.sum(ahead * hot_f, axis=0, keepdims=True).astype(jnp.int32)
    chunk_of = jnp.sum(hot_f * chunk.astype(jnp.float32), axis=0, keepdims=True).astype(jnp.int32)
    slot_of = chunk_of * CAP + rank
    count = jnp.sum(hot_f, axis=1, keepdims=True)

    load.wait()
    raw = emb[...]
    norm = jnp.sum(raw * raw, axis=-1, keepdims=True)
    unit[...] = (raw * lax.rsqrt(norm + 1e-06)).astype(jnp.bfloat16)

    def dispatch(k):
        return pltpu.make_async_remote_copy(
            src_ref=outgoing.at[k],
            dst_ref=own.at[k],
            send_sem=send_sem.at[k],
            recv_sem=recv_sem.at[k],
            device_id={"dev": target(k)},
            device_id_type=MESH,
        )

    def start_dispatch(k, carry):
        dispatch(k).start()
        return carry

    def to_relay(i):
        z = (mez + (1, nz - 1)[i]) % nz
        return pltpu.make_async_remote_copy(
            src_ref=outgoing.at[RELAYED[i]],
            dst_ref=relay.at[i],
            send_sem=send_sem.at[RELAYED[i]],
            recv_sem=relay_recv.at[i],
            device_id={"dev": 2 * z + mec},
            device_id_type=MESH,
        )

    def from_relay(i):
        z = (mez + (nz // 2 - 1, nz // 2 + 1)[i]) % nz
        return pltpu.make_async_remote_copy(
            src_ref=relay.at[i],
            dst_ref=own.at[RELAYED[i]],
            send_sem=relay_send.at[i],
            recv_sem=recv_sem.at[RELAYED[i]],
            device_id={"dev": 2 * z + (mec + RELAYED[i]) % 2},
            device_id_type=MESH,
        )

    slot = lax.broadcasted_iota(jnp.int32, (PACK * CAP, 1), 0)
    first = lax.broadcasted_iota(jnp.int32, (CAP, width), 1) == 0
    in_chunk = lax.broadcasted_iota(jnp.int32, (CAP, width), 0).astype(jnp.float32)
    for t in range(owners // PACK):
        pick = jnp.where(slot_of == slot + t * PACK * CAP, 1.0, 0.0).astype(jnp.bfloat16)
        packed = jnp.dot(pick, unit[...], preferred_element_type=jnp.float32)
        for c in range(PACK):
            k = t * PACK + c
            empty = first & (in_chunk >= count[k : k + 1, :])
            piece = jnp.where(empty, DEAD, packed[c * CAP : (c + 1) * CAP, :]).astype(jnp.bfloat16)
            if k == here:
                own[k] = piece
            else:
                outgoing[k] = piece
        if t == 0:
            pl.semaphore_wait(barrier, owners + 1)
            to_relay(0).start()
            to_relay(1).start()
            dispatch(1).start()
        else:
            lax.fori_loop(t * PACK, (t + 1) * PACK, start_dispatch, 0)
        if t == owners // PACK // 2:
            for i in range(2):
                to_relay(i).wait_recv()
                from_relay(i).start()

    acc[...] = jnp.full_like(acc, -4.0)

    def forward(p, way):
        part = pl.ds(p * PIECE, PIECE)
        return pltpu.make_async_remote_copy(
            src_ref=own.at[part],
            dst_ref=(before if way == 0 else after).at[part],
            send_sem=pair_send.at[way, p],
            recv_sem=pair_recv.at[way, p],
            device_id={"group": later if way == 0 else earlier},
            device_id_type=MESH,
        )

    def block(which, found, jb, ib, diagonal=False):
        right = found[pl.ds(jb * STAGE, STAGE)].reshape(STAGE * CAP, width)
        left = own[pl.ds(ib * STAGE, STAGE)].reshape(STAGE * CAP, width)
        scores = lax.dot_general(right, left, (((1,), (1,)), ((), ())), preferred_element_type=jnp.float32)
        drop = right[:, :128].astype(jnp.float32)[:, 0:1] > 1.5
        if diagonal:
            size = STAGE * CAP
            drop = drop | (
                lax.broadcasted_iota(jnp.int32, (size, size), 0) == lax.broadcasted_iota(jnp.int32, (size, size), 1)
            )
        scores = jnp.where(drop, -1.0, scores)
        best = jnp.max(scores.reshape(STAGE * CAP // 8, 8, STAGE * CAP), axis=0)
        acc[which, ib] = jnp.maximum(acc[which, ib], best)

    def arrive(t):
        def chunk_arrives(k, carry):
            dispatch(k).wait_recv()
            return carry

        def piece_arrives(p, carry):
            lax.fori_loop(p * PIECE, (p + 1) * PIECE, chunk_arrives, 0)
            forward(p, 0).start()
            forward(p, 1).start()
            return carry

        per = STAGE // PIECE
        if t == 0:
            lax.fori_loop(1, PIECE, chunk_arrives, 0)
            forward(0, 0).start()
            forward(0, 1).start()
            lax.fori_loop(1, per, piece_arrives, 0)
        else:
            lax.fori_loop(t * per, (t + 1) * per, piece_arrives, 0)

    def pair_arrives(t):
        def piece(p, carry):
            forward(p, 0).wait_recv()
            forward(p, 1).wait_recv()
            return carry

        per = STAGE // PIECE
        lax.fori_loop(t * per, (t + 1) * per, piece, 0)

    def both(jb, ib):
        block(1, after, jb, ib)
        block(2, before, jb, ib)

    for t in range(stages):
        arrive(t)
        block(0, own, t, t, diagonal=True)

        def own_blocks(b, carry, t=t):
            block(0, own, t, b)
            block(0, own, b, t)
            return carry

        lax.fori_loop(0, t, own_blocks, 0)
        if t > 0:
            pair_arrives(t - 1)

            def new_rows(b, carry, t=t):
                both(b, t)
                return carry

            def new_found(b, carry, t=t):
                both(t - 1, b)
                return carry

            lax.fori_loop(0, t, new_rows, 0)
            lax.fori_loop(0, t, new_found, 0)
    pair_arrives(stages - 1)

    def last_found(b, carry):
        both(stages - 1, b)
        return carry

    lax.fori_loop(0, stages, last_found, 0)

    tiles = []
    for which in range(3):
        parts = []
        for b in range(stages):
            best = jnp.max(acc[which, b], axis=0, keepdims=True)
            parts += [best[:, h * 128 : (h + 1) * 128] for h in range(STAGE * CAP // 128)]
        tiles.append(jnp.concatenate(parts, axis=0))
    lane = lax.broadcasted_iota(jnp.int32, tiles[0].shape, 1)
    per_tile = 128 // CAP
    for j in range(per_tile):
        moved = [pltpu.roll(tiles[w], (CAP * (w - j)) % 128, 1) if (w - j) % 4 else tiles[w] for w in range(3)]
        mixed = jnp.where(lane < CAP, moved[0], jnp.where(lane < 2 * CAP, moved[1], moved[2]))
        for t in range(owners // per_tile):
            k = per_tile * t + j
            if k == here:
                got[k] = mixed[t : t + 1, :]
            else:
                ret[k] = mixed[t : t + 1, :]

    def give_back(k):
        return pltpu.make_async_remote_copy(
            src_ref=ret.at[k],
            dst_ref=got.at[k],
            send_sem=ret_send.at[k],
            recv_sem=ret_recv.at[k],
            device_id={"dev": source(k)},
            device_id_type=MESH,
        )

    def start_back(k, carry):
        give_back(k).start()
        return carry

    lax.fori_loop(2, owners, start_back, 0)
    give_back(1).start()

    def drain(k, carry):
        dispatch(k).wait_send()
        return carry

    lax.fori_loop(1, owners, drain, 0)
    for i in range(2):
        from_relay(i).wait_send()

    def drain_pair(p, carry):
        forward(p, 0).wait_send()
        forward(p, 1).wait_send()
        return carry

    lax.fori_loop(0, owners // PIECE, drain_pair, 0)

    def wait_back(k, carry):
        give_back(k).wait()
        return carry

    lax.fori_loop(1, owners, wait_back, 0)

    table = got[...].reshape(owners, 128)
    high = table.astype(jnp.bfloat16)
    rest = table - high.astype(jnp.float32)
    middle = rest.astype(jnp.bfloat16)
    low = (rest - middle.astype(jnp.float32)).astype(jnp.bfloat16)
    stacked = jnp.concatenate([high, middle, low], axis=0)
    picks = jnp.concatenate([hot_b, hot_b, hot_b], axis=0)
    found = lax.dot_general(stacked, picks, (((0,), (0,)), ((), ())), preferred_element_type=jnp.float32)
    mine = lax.broadcasted_iota(jnp.int32, (CAP, 1), 0) == rank
    for which in range(3):
        kept = jnp.where(mine, found[which * CAP : (which + 1) * CAP, :], 0.0)
        line = jnp.sum(kept, axis=0, keepdims=True)
        for a in range(rows // 128):
            out_ref[which, a : a + 1, :] = line[:, a * 128 : (a + 1) * 128]


def local(embeddings, owner):
    owners = lax.axis_size("dev")
    groups = lax.axis_size("group")
    rows, width = embeddings.shape
    vmem = pl.BlockSpec(memory_space=pltpu.VMEM)
    slots = (owners, CAP, width)
    hbm = pl.BlockSpec(memory_space=pltpu.HBM)
    out = pl.pallas_call(
        functools.partial(kernel, groups=groups, owners=owners),
        out_shape=jax.ShapeDtypeStruct((3, rows // 128, 128), jnp.float32),
        in_specs=[hbm, hbm],
        out_specs=vmem,
        scratch_shapes=[
            pltpu.VMEM((rows, width), jnp.float32),
            pltpu.VMEM((rows // 128, 128), jnp.int32),
            pltpu.VMEM((rows, width), jnp.bfloat16),
            pltpu.VMEM(slots, jnp.bfloat16),
            pltpu.VMEM(slots, jnp.bfloat16),
            pltpu.VMEM(slots, jnp.bfloat16),
            pltpu.VMEM(slots, jnp.bfloat16),
            pltpu.VMEM((3, owners // STAGE, 8, STAGE * CAP), jnp.float32),
            pltpu.VMEM((owners, 1, 128), jnp.float32),
            pltpu.VMEM((owners, 1, 128), jnp.float32),
            pltpu.VMEM((2, CAP, width), jnp.bfloat16),
            pltpu.SemaphoreType.DMA((2,)),
            pltpu.SemaphoreType.DMA((owners,)),
            pltpu.SemaphoreType.DMA((owners,)),
            pltpu.SemaphoreType.DMA((2, owners // PIECE)),
            pltpu.SemaphoreType.DMA((2, owners // PIECE)),
            pltpu.SemaphoreType.DMA((owners,)),
            pltpu.SemaphoreType.DMA((owners,)),
            pltpu.SemaphoreType.DMA((2,)),
            pltpu.SemaphoreType.DMA((2,)),
        ],
        compiler_params=pltpu.CompilerParams(
            collective_id=0, has_side_effects=True, vmem_limit_bytes=60 * 1024 * 1024
        ),
    )(embeddings, owner.reshape(rows // 128, 128))
    return tuple(out[which].reshape(rows) for which in range(3))


def solution(mesh):
    placed = (P(("group", "dev"), None), P(("group", "dev")))
    return jax.shard_map(
        local,
        mesh=mesh,
        in_specs=placed,
        out_specs=(P(("group", "dev")), P(("group", "dev")), P(("group", "dev"))),
        check_vma=False,
    )
```

```python
import functools

import jax
import jax.numpy as jnp
from jax import lax
from jax.experimental import pallas as pl
from jax.experimental.pallas import tpu as pltpu
from jax.sharding import PartitionSpec as P

CAP = 32
DEAD = 2.0
STAGE = 8
PIECE = 1
PACK = 4
MESH = pl.DeviceIdType.MESH


def ring_offset(k, nz):
    j = k // 2
    size = (j + 1) // 2
    return jnp.where(j % 2 == 1, size, -size)


def kernel(
    emb_hbm,
    owner_hbm,
    out_ref,
    emb,
    owner_ref,
    unit,
    outgoing,
    own,
    before,
    after,
    acc,
    ret,
    got,
    load_sem,
    send_sem,
    recv_sem,
    pair_send,
    pair_recv,
    ret_send,
    ret_recv,
    *,
    groups,
    owners,
):
    rows, width = emb.shape
    nz = owners // 2
    group = lax.axis_index("group")
    me = lax.axis_index("dev")
    mez, mec = me // 2, me % 2
    stages = owners // STAGE
    here = 0

    load_owner = pltpu.make_async_copy(owner_hbm, owner_ref, load_sem.at[0])
    load_owner.start()
    load = pltpu.make_async_copy(emb_hbm, emb, load_sem.at[1])
    load.start()

    def target(k):
        z = (mez + ring_offset(k, nz) + nz) % nz
        return 2 * z + (mec + k) % 2

    def source(k):
        z = (mez - ring_offset(k, nz) + nz) % nz
        return 2 * z + (mec + k) % 2

    barrier = pltpu.get_barrier_semaphore()

    def greet(d, carry):
        pl.semaphore_signal(barrier, inc=1, device_id={"dev": (me + d) % owners}, device_id_type=MESH)
        return carry

    lax.fori_loop(1, owners, greet, 0)
    later = (group + 1) % groups
    earlier = (group + groups - 1) % groups
    pl.semaphore_signal(barrier, inc=1, device_id={"group": later}, device_id_type=MESH)
    pl.semaphore_signal(barrier, inc=1, device_id={"group": earlier}, device_id_type=MESH)

    load_owner.wait()

    owner = jnp.concatenate([owner_ref[a : a + 1, :] for a in range(rows // 128)], axis=1)
    chunk = lax.broadcasted_iota(jnp.int32, (owners, 1), 0)
    cluster = 2 * ((mez + ring_offset(chunk, nz) + nz) % nz) + (mec + chunk) % 2
    hot = owner == cluster
    hot_f = jnp.where(hot, 1.0, 0.0)
    hot_b = hot_f.astype(jnp.bfloat16)
    earlier_row = lax.broadcasted_iota(jnp.int32, (rows, rows), 0) < lax.broadcasted_iota(
        jnp.int32, (rows, rows), 1
    )
    ahead = jnp.dot(
        hot_b, jnp.where(earlier_row, 1.0, 0.0).astype(jnp.bfloat16), preferred_element_type=jnp.float32
    )
    rank = jnp.sum(ahead * hot_f, axis=0, keepdims=True).astype(jnp.int32)
    chunk_of = jnp.sum(hot_f * chunk.astype(jnp.float32), axis=0, keepdims=True).astype(jnp.int32)
    slot_of = chunk_of * CAP + rank
    count = jnp.sum(hot_f, axis=1, keepdims=True)

    load.wait()
    raw = emb[...]
    norm = jnp.sum(raw * raw, axis=-1, keepdims=True)
    unit[...] = (raw * lax.rsqrt(norm + 1e-06)).astype(jnp.bfloat16)

    def dispatch(k):
        return pltpu.make_async_remote_copy(
            src_ref=outgoing.at[k],
            dst_ref=own.at[k],
            send_sem=send_sem.at[k],
            recv_sem=recv_sem.at[k],
            device_id={"dev": target(k)},
            device_id_type=MESH,
        )

    def start_dispatch(k, carry):
        dispatch(k).start()
        return carry

    slot = lax.broadcasted_iota(jnp.int32, (PACK * CAP, 1), 0)
    first = lax.broadcasted_iota(jnp.int32, (CAP, width), 1) == 0
    in_chunk = lax.broadcasted_iota(jnp.int32, (CAP, width), 0).astype(jnp.float32)
    for t in range(owners // PACK):
        pick = jnp.where(slot_of == slot + t * PACK * CAP, 1.0, 0.0).astype(jnp.bfloat16)
        packed = jnp.dot(pick, unit[...], preferred_element_type=jnp.float32)
        for c in range(PACK):
            k = t * PACK + c
            empty = first & (in_chunk >= count[k : k + 1, :])
            piece = jnp.where(empty, DEAD, packed[c * CAP : (c + 1) * CAP, :]).astype(jnp.bfloat16)
            if k == here:
                own[k] = piece
            else:
                outgoing[k] = piece
        if t == 0:
            pl.semaphore_wait(barrier, owners + 1)
        lax.fori_loop(max(t * PACK, 1), (t + 1) * PACK, start_dispatch, 0)

    acc[...] = jnp.full_like(acc, -4.0)

    def forward(p, way):
        part = pl.ds(p * PIECE, PIECE)
        return pltpu.make_async_remote_copy(
            src_ref=own.at[part],
            dst_ref=(before if way == 0 else after).at[part],
            send_sem=pair_send.at[way, p],
            recv_sem=pair_recv.at[way, p],
            device_id={"group": later if way == 0 else earlier},
            device_id_type=MESH,
        )

    def block(which, found, jb, ib, diagonal=False):
        right = found[pl.ds(jb * STAGE, STAGE)].reshape(STAGE * CAP, width)
        left = own[pl.ds(ib * STAGE, STAGE)].reshape(STAGE * CAP, width)
        scores = lax.dot_general(right, left, (((1,), (1,)), ((), ())), preferred_element_type=jnp.float32)
        drop = right[:, :128].astype(jnp.float32)[:, 0:1] > 1.5
        if diagonal:
            size = STAGE * CAP
            drop = drop | (
                lax.broadcasted_iota(jnp.int32, (size, size), 0) == lax.broadcasted_iota(jnp.int32, (size, size), 1)
            )
        scores = jnp.where(drop, -1.0, scores)
        best = jnp.max(scores.reshape(STAGE * CAP // 8, 8, STAGE * CAP), axis=0)
        acc[which, ib] = jnp.maximum(acc[which, ib], best)

    def arrive(t):
        def chunk_arrives(k, carry):
            dispatch(k).wait_recv()
            return carry

        def piece_arrives(p, carry):
            lax.fori_loop(p * PIECE, (p + 1) * PIECE, chunk_arrives, 0)
            forward(p, 0).start()
            forward(p, 1).start()
            return carry

        per = STAGE // PIECE
        if t == 0:
            lax.fori_loop(1, PIECE, chunk_arrives, 0)
            forward(0, 0).start()
            forward(0, 1).start()
            lax.fori_loop(1, per, piece_arrives, 0)
        else:
            lax.fori_loop(t * per, (t + 1) * per, piece_arrives, 0)

    def pair_arrives(t):
        def piece(p, carry):
            forward(p, 0).wait_recv()
            forward(p, 1).wait_recv()
            return carry

        per = STAGE // PIECE
        lax.fori_loop(t * per, (t + 1) * per, piece, 0)

    def both(jb, ib):
        block(1, after, jb, ib)
        block(2, before, jb, ib)

    for t in range(stages):
        arrive(t)
        block(0, own, t, t, diagonal=True)

        def own_blocks(b, carry, t=t):
            block(0, own, t, b)
            block(0, own, b, t)
            return carry

        lax.fori_loop(0, t, own_blocks, 0)
        if t > 0:
            pair_arrives(t - 1)

            def new_rows(b, carry, t=t):
                both(b, t)
                return carry

            def new_found(b, carry, t=t):
                both(t - 1, b)
                return carry

            lax.fori_loop(0, t, new_rows, 0)
            lax.fori_loop(0, t, new_found, 0)
    pair_arrives(stages - 1)

    def last_found(b, carry):
        both(stages - 1, b)
        return carry

    lax.fori_loop(0, stages, last_found, 0)

    tiles = []
    for which in range(3):
        parts = []
        for b in range(stages):
            best = jnp.max(acc[which, b], axis=0, keepdims=True)
            parts += [best[:, h * 128 : (h + 1) * 128] for h in range(STAGE * CAP // 128)]
        tiles.append(jnp.concatenate(parts, axis=0))
    lane = lax.broadcasted_iota(jnp.int32, tiles[0].shape, 1)
    per_tile = 128 // CAP
    for j in range(per_tile):
        moved = [pltpu.roll(tiles[w], (CAP * (w - j)) % 128, 1) if (w - j) % 4 else tiles[w] for w in range(3)]
        mixed = jnp.where(lane < CAP, moved[0], jnp.where(lane < 2 * CAP, moved[1], moved[2]))
        for t in range(owners // per_tile):
            k = per_tile * t + j
            if k == here:
                got[k] = mixed[t : t + 1, :]
            else:
                ret[k] = mixed[t : t + 1, :]

    def give_back(k):
        return pltpu.make_async_remote_copy(
            src_ref=ret.at[k],
            dst_ref=got.at[k],
            send_sem=ret_send.at[k],
            recv_sem=ret_recv.at[k],
            device_id={"dev": source(k)},
            device_id_type=MESH,
        )

    def start_back(k, carry):
        give_back(k).start()
        return carry

    lax.fori_loop(1, owners, start_back, 0)

    def drain(k, carry):
        dispatch(k).wait_send()
        return carry

    lax.fori_loop(1, owners, drain, 0)

    def drain_pair(p, carry):
        forward(p, 0).wait_send()
        forward(p, 1).wait_send()
        return carry

    lax.fori_loop(0, owners // PIECE, drain_pair, 0)

    def wait_back(k, carry):
        give_back(k).wait()
        return carry

    lax.fori_loop(1, owners, wait_back, 0)

    table = got[...].reshape(owners, 128)
    high = table.astype(jnp.bfloat16)
    rest = table - high.astype(jnp.float32)
    middle = rest.astype(jnp.bfloat16)
    low = (rest - middle.astype(jnp.float32)).astype(jnp.bfloat16)
    stacked = jnp.concatenate([high, middle, low], axis=0)
    picks = jnp.concatenate([hot_b, hot_b, hot_b], axis=0)
    found = lax.dot_general(stacked, picks, (((0,), (0,)), ((), ())), preferred_element_type=jnp.float32)
    mine = lax.broadcasted_iota(jnp.int32, (CAP, 1), 0) == rank
    for which in range(3):
        kept = jnp.where(mine, found[which * CAP : (which + 1) * CAP, :], 0.0)
        line = jnp.sum(kept, axis=0, keepdims=True)
        for a in range(rows // 128):
            out_ref[which, a : a + 1, :] = line[:, a * 128 : (a + 1) * 128]


def local(embeddings, owner):
    owners = lax.axis_size("dev")
    groups = lax.axis_size("group")
    rows, width = embeddings.shape
    vmem = pl.BlockSpec(memory_space=pltpu.VMEM)
    slots = (owners, CAP, width)
    hbm = pl.BlockSpec(memory_space=pltpu.HBM)
    out = pl.pallas_call(
        functools.partial(kernel, groups=groups, owners=owners),
        out_shape=jax.ShapeDtypeStruct((3, rows // 128, 128), jnp.float32),
        in_specs=[hbm, hbm],
        out_specs=vmem,
        scratch_shapes=[
            pltpu.VMEM((rows, width), jnp.float32),
            pltpu.VMEM((rows // 128, 128), jnp.int32),
            pltpu.VMEM((rows, width), jnp.bfloat16),
            pltpu.VMEM(slots, jnp.bfloat16),
            pltpu.VMEM(slots, jnp.bfloat16),
            pltpu.VMEM(slots, jnp.bfloat16),
            pltpu.VMEM(slots, jnp.bfloat16),
            pltpu.VMEM((3, owners // STAGE, 8, STAGE * CAP), jnp.float32),
            pltpu.VMEM((owners, 1, 128), jnp.float32),
            pltpu.VMEM((owners, 1, 128), jnp.float32),
            pltpu.SemaphoreType.DMA((2,)),
            pltpu.SemaphoreType.DMA((owners,)),
            pltpu.SemaphoreType.DMA((owners,)),
            pltpu.SemaphoreType.DMA((2, owners // PIECE)),
            pltpu.SemaphoreType.DMA((2, owners // PIECE)),
            pltpu.SemaphoreType.DMA((owners,)),
            pltpu.SemaphoreType.DMA((owners,)),
        ],
        compiler_params=pltpu.CompilerParams(
            collective_id=0, has_side_effects=True, vmem_limit_bytes=60 * 1024 * 1024
        ),
    )(embeddings, owner.reshape(rows // 128, 128))
    return tuple(out[which].reshape(rows) for which in range(3))


def solution(mesh):
    placed = (P(("group", "dev"), None), P(("group", "dev")))
    return jax.shard_map(
        local,
        mesh=mesh,
        in_specs=placed,
        out_specs=(P(("group", "dev")), P(("group", "dev")), P(("group", "dev"))),
        check_vma=False,
    )
```

```python
import functools

import jax
import jax.numpy as jnp
from jax import lax
from jax.experimental import pallas as pl
from jax.experimental.pallas import tpu as pltpu
from jax.sharding import PartitionSpec as P

CAP = 32
DEAD = 2.0
STAGE = 8
PIECE = 1
PACK = 4
BASE = 16
POOL = 64
FULL = 1000.0
LEAD = 8
MESH = pl.DeviceIdType.MESH


def ring_offset(k, nz):
    j = k // 2
    size = (j + 1) // 2
    return jnp.where(j % 2 == 1, size, -size)


def padded(
    emb_hbm,
    owner_hbm,
    out_ref,
    emb,
    owner_ref,
    unit,
    outgoing,
    own,
    before,
    after,
    acc,
    ret,
    got,
    load_sem,
    send_sem,
    recv_sem,
    pair_send,
    pair_recv,
    ret_send,
    ret_recv,
    *,
    groups,
    owners,
):
    rows, width = emb.shape
    nz = owners // 2
    group = lax.axis_index("group")
    me = lax.axis_index("dev")
    mez, mec = me // 2, me % 2
    stages = owners // STAGE
    here = 0

    load_owner = pltpu.make_async_copy(owner_hbm, owner_ref, load_sem.at[0])
    load_owner.start()
    load = pltpu.make_async_copy(emb_hbm, emb, load_sem.at[1])
    load.start()

    def target(k):
        z = (mez + ring_offset(k, nz) + nz) % nz
        return 2 * z + (mec + k) % 2

    def source(k):
        z = (mez - ring_offset(k, nz) + nz) % nz
        return 2 * z + (mec + k) % 2

    barrier = pltpu.get_barrier_semaphore()

    def greet(d, carry):
        pl.semaphore_signal(barrier, inc=1, device_id={"dev": (me + d) % owners}, device_id_type=MESH)
        return carry

    lax.fori_loop(1, owners, greet, 0)
    later = (group + 1) % groups
    earlier = (group + groups - 1) % groups
    pl.semaphore_signal(barrier, inc=1, device_id={"group": later}, device_id_type=MESH)
    pl.semaphore_signal(barrier, inc=1, device_id={"group": earlier}, device_id_type=MESH)

    load_owner.wait()

    owner = jnp.concatenate([owner_ref[a : a + 1, :] for a in range(rows // 128)], axis=1)
    chunk = lax.broadcasted_iota(jnp.int32, (owners, 1), 0)
    cluster = 2 * ((mez + ring_offset(chunk, nz) + nz) % nz) + (mec + chunk) % 2
    hot = owner == cluster
    hot_f = jnp.where(hot, 1.0, 0.0)
    hot_b = hot_f.astype(jnp.bfloat16)
    earlier_row = lax.broadcasted_iota(jnp.int32, (rows, rows), 0) < lax.broadcasted_iota(
        jnp.int32, (rows, rows), 1
    )
    ahead = jnp.dot(
        hot_b, jnp.where(earlier_row, 1.0, 0.0).astype(jnp.bfloat16), preferred_element_type=jnp.float32
    )
    rank = jnp.sum(ahead * hot_f, axis=0, keepdims=True).astype(jnp.int32)
    chunk_of = jnp.sum(hot_f * chunk.astype(jnp.float32), axis=0, keepdims=True).astype(jnp.int32)
    slot_of = chunk_of * CAP + rank
    count = jnp.sum(hot_f, axis=1, keepdims=True)

    load.wait()
    raw = emb[...]
    norm = jnp.sum(raw * raw, axis=-1, keepdims=True)
    unit[...] = (raw * lax.rsqrt(norm + 1e-06)).astype(jnp.bfloat16)

    def dispatch(k):
        return pltpu.make_async_remote_copy(
            src_ref=outgoing.at[k],
            dst_ref=own.at[k],
            send_sem=send_sem.at[k],
            recv_sem=recv_sem.at[k],
            device_id={"dev": target(k)},
            device_id_type=MESH,
        )

    def start_dispatch(k, carry):
        dispatch(k).start()
        return carry

    slot = lax.broadcasted_iota(jnp.int32, (PACK * CAP, 1), 0)
    first = lax.broadcasted_iota(jnp.int32, (CAP, width), 1) == 0
    in_chunk = lax.broadcasted_iota(jnp.int32, (CAP, width), 0).astype(jnp.float32)
    for t in range(owners // PACK):
        pick = jnp.where(slot_of == slot + t * PACK * CAP, 1.0, 0.0).astype(jnp.bfloat16)
        packed = jnp.dot(pick, unit[...], preferred_element_type=jnp.float32)
        for c in range(PACK):
            k = t * PACK + c
            empty = first & (in_chunk >= count[k : k + 1, :])
            piece = jnp.where(empty, DEAD, packed[c * CAP : (c + 1) * CAP, :]).astype(jnp.bfloat16)
            if k == here:
                own[k] = piece
            else:
                outgoing[k] = piece
        if t == 0:
            pl.semaphore_wait(barrier, owners + 1)
        lax.fori_loop(max(t * PACK, 1), (t + 1) * PACK, start_dispatch, 0)

    acc[...] = jnp.full_like(acc, -4.0)

    def forward(p, way):
        part = pl.ds(p * PIECE, PIECE)
        return pltpu.make_async_remote_copy(
            src_ref=own.at[part],
            dst_ref=(before if way == 0 else after).at[part],
            send_sem=pair_send.at[way, p],
            recv_sem=pair_recv.at[way, p],
            device_id={"group": later if way == 0 else earlier},
            device_id_type=MESH,
        )

    def block(which, found, jb, ib, diagonal=False):
        right = found[pl.ds(jb * STAGE, STAGE)].reshape(STAGE * CAP, width)
        left = own[pl.ds(ib * STAGE, STAGE)].reshape(STAGE * CAP, width)
        scores = lax.dot_general(right, left, (((1,), (1,)), ((), ())), preferred_element_type=jnp.float32)
        drop = right[:, :128].astype(jnp.float32)[:, 0:1] > 1.5
        if diagonal:
            size = STAGE * CAP
            drop = drop | (
                lax.broadcasted_iota(jnp.int32, (size, size), 0) == lax.broadcasted_iota(jnp.int32, (size, size), 1)
            )
        scores = jnp.where(drop, -1.0, scores)
        best = jnp.max(scores.reshape(STAGE * CAP // 8, 8, STAGE * CAP), axis=0)
        acc[which, ib] = jnp.maximum(acc[which, ib], best)

    def arrive(t):
        def chunk_arrives(k, carry):
            dispatch(k).wait_recv()
            return carry

        def piece_arrives(p, carry):
            lax.fori_loop(p * PIECE, (p + 1) * PIECE, chunk_arrives, 0)
            forward(p, 0).start()
            forward(p, 1).start()
            return carry

        per = STAGE // PIECE
        if t == 0:
            lax.fori_loop(1, PIECE, chunk_arrives, 0)
            forward(0, 0).start()
            forward(0, 1).start()
            lax.fori_loop(1, per, piece_arrives, 0)
        else:
            lax.fori_loop(t * per, (t + 1) * per, piece_arrives, 0)

    def pair_arrives(t):
        def piece(p, carry):
            forward(p, 0).wait_recv()
            forward(p, 1).wait_recv()
            return carry

        per = STAGE // PIECE
        lax.fori_loop(t * per, (t + 1) * per, piece, 0)

    def both(jb, ib):
        block(1, after, jb, ib)
        block(2, before, jb, ib)

    for t in range(stages):
        arrive(t)
        block(0, own, t, t, diagonal=True)

        def own_blocks(b, carry, t=t):
            block(0, own, t, b)
            block(0, own, b, t)
            return carry

        lax.fori_loop(0, t, own_blocks, 0)
        if t > 0:
            pair_arrives(t - 1)

            def new_rows(b, carry, t=t):
                both(b, t)
                return carry

            def new_found(b, carry, t=t):
                both(t - 1, b)
                return carry

            lax.fori_loop(0, t, new_rows, 0)
            lax.fori_loop(0, t, new_found, 0)
    pair_arrives(stages - 1)

    def last_found(b, carry):
        both(stages - 1, b)
        return carry

    lax.fori_loop(0, stages, last_found, 0)

    tiles = []
    for which in range(3):
        parts = []
        for b in range(stages):
            best = jnp.max(acc[which, b], axis=0, keepdims=True)
            parts += [best[:, h * 128 : (h + 1) * 128] for h in range(STAGE * CAP // 128)]
        tiles.append(jnp.concatenate(parts, axis=0))
    lane = lax.broadcasted_iota(jnp.int32, tiles[0].shape, 1)
    per_tile = 128 // CAP
    for j in range(per_tile):
        moved = [pltpu.roll(tiles[w], (CAP * (w - j)) % 128, 1) if (w - j) % 4 else tiles[w] for w in range(3)]
        mixed = jnp.where(lane < CAP, moved[0], jnp.where(lane < 2 * CAP, moved[1], moved[2]))
        for t in range(owners // per_tile):
            k = per_tile * t + j
            if k == here:
                got[k] = mixed[t : t + 1, :]
            else:
                ret[k] = mixed[t : t + 1, :]

    def give_back(k):
        return pltpu.make_async_remote_copy(
            src_ref=ret.at[k],
            dst_ref=got.at[k],
            send_sem=ret_send.at[k],
            recv_sem=ret_recv.at[k],
            device_id={"dev": source(k)},
            device_id_type=MESH,
        )

    def start_back(k, carry):
        give_back(k).start()
        return carry

    lax.fori_loop(1, owners, start_back, 0)

    def drain(k, carry):
        dispatch(k).wait_send()
        return carry

    lax.fori_loop(1, owners, drain, 0)

    def drain_pair(p, carry):
        forward(p, 0).wait_send()
        forward(p, 1).wait_send()
        return carry

    lax.fori_loop(0, owners // PIECE, drain_pair, 0)

    def wait_back(k, carry):
        give_back(k).wait()
        return carry

    lax.fori_loop(1, owners, wait_back, 0)

    table = got[...].reshape(owners, 128)
    high = table.astype(jnp.bfloat16)
    rest = table - high.astype(jnp.float32)
    middle = rest.astype(jnp.bfloat16)
    low = (rest - middle.astype(jnp.float32)).astype(jnp.bfloat16)
    stacked = jnp.concatenate([high, middle, low], axis=0)
    picks = jnp.concatenate([hot_b, hot_b, hot_b], axis=0)
    found = lax.dot_general(stacked, picks, (((0,), (0,)), ((), ())), preferred_element_type=jnp.float32)
    mine = lax.broadcasted_iota(jnp.int32, (CAP, 1), 0) == rank
    for which in range(3):
        kept = jnp.where(mine, found[which * CAP : (which + 1) * CAP, :], 0.0)
        line = jnp.sum(kept, axis=0, keepdims=True)
        for a in range(rows // 128):
            out_ref[which, a : a + 1, :] = line[:, a * 128 : (a + 1) * 128]


def pooled(
    emb_hbm,
    owner_hbm,
    out_ref,
    flag_ref,
    emb,
    owner_ref,
    unit,
    outgoing,
    side,
    own,
    before,
    after,
    acc,
    ret,
    got,
    pool_out,
    pool,
    key_out,
    keys,
    full,
    load_sem,
    send_sem,
    recv_sem,
    pair_send,
    pair_recv,
    ret_send,
    ret_recv,
    hop_send,
    hop_recv,
    share_send,
    share_recv,
    key_hop_send,
    key_hop_recv,
    key_share_send,
    key_share_recv,
    full_send,
    full_recv,
    side_send,
    side_recv,
    *,
    groups,
    owners,
):
    rows, width = emb.shape
    nz = owners // 2
    group = lax.axis_index("group")
    me = lax.axis_index("dev")
    mez, mec = me // 2, me % 2
    sibling = 2 * mez + 1 - mec
    steps = nz // 2
    per_block = STAGE * CAP // BASE
    blocks = 2 * owners // per_block

    load_owner = pltpu.make_async_copy(owner_hbm, owner_ref, load_sem.at[0])
    load_owner.start()
    load = pltpu.make_async_copy(emb_hbm, emb, load_sem.at[1])
    load.start()

    def target(k):
        return 2 * ((mez + ring_offset(k, nz) + nz) % nz) + (mec + k) % 2

    def source(k):
        return 2 * ((mez - ring_offset(k, nz) + nz) % nz) + (mec + k) % 2

    barrier = pltpu.get_barrier_semaphore()

    def greet(d, carry):
        pl.semaphore_signal(barrier, inc=1, device_id={"dev": (me + d) % owners}, device_id_type=MESH)
        return carry

    def greet_group(d, carry):
        pl.semaphore_signal(barrier, inc=1, device_id={"group": (group + d) % groups}, device_id_type=MESH)
        return carry

    lax.fori_loop(1, owners, greet, 0)
    lax.fori_loop(1, groups, greet_group, 0)

    load_owner.wait()
    owner = jnp.concatenate([owner_ref[a : a + 1, :] for a in range(rows // 128)], axis=1)
    chunk = lax.broadcasted_iota(jnp.int32, (owners, 1), 0)
    cluster = 2 * ((mez + ring_offset(chunk, nz) + nz) % nz) + (mec + chunk) % 2
    hot_f = jnp.where(owner == cluster, 1.0, 0.0)
    hot_b = hot_f.astype(jnp.bfloat16)
    earlier_row = lax.broadcasted_iota(jnp.int32, (rows, rows), 0) < lax.broadcasted_iota(
        jnp.int32, (rows, rows), 1
    )
    ahead = jnp.dot(
        hot_b, jnp.where(earlier_row, 1.0, 0.0).astype(jnp.bfloat16), preferred_element_type=jnp.float32
    )

    def of_row(per_chunk):
        return jnp.sum(hot_f * per_chunk, axis=0, keepdims=True).astype(jnp.int32)

    rank = of_row(ahead)
    chunk_of = of_row(chunk.astype(jnp.float32))
    count = jnp.sum(hot_f, axis=1, keepdims=True)
    counts = lax.dot_general(
        jnp.ones((8, rows), jnp.bfloat16), hot_b, (((1,), (1,)), ((), ())), preferred_element_type=jnp.float32
    )[0:1, :]

    lane = lax.broadcasted_iota(jnp.int32, (1, owners), 1)
    spill = jnp.where(lane >= 2, jnp.maximum(counts - BASE, 0.0), 0.0)

    def way_of(k):
        return 1 - (k // 2) % 2

    same_way = way_of(lane) == way_of(chunk)
    start = jnp.sum(jnp.where(same_way & (lane < chunk), spill, 0.0), axis=1, keepdims=True)
    most = jnp.max(jnp.sum(jnp.where(same_way, spill, 0.0), axis=1, keepdims=True), axis=0, keepdims=True)
    at = of_row(start) + rank - BASE
    spilled = (rank >= BASE) & (chunk_of >= 2) & (at < POOL)
    pool_slot = jnp.where(spilled, way_of(chunk_of) * POOL + at, -1)
    hops = (chunk_of // 2 + 1) // 2
    key = jnp.where(spilled, ((hops - 1) * 2 + chunk_of % 2) * BASE + rank - BASE + 1, 0)
    base_slot = jnp.where(rank < BASE, chunk_of * BASE + rank, -1)
    side_slot = jnp.where((rank >= BASE) & (chunk_of < 2), chunk_of * BASE + rank - BASE, -1)

    def pick(slot_of, count_, start_=0):
        slot = lax.broadcasted_iota(jnp.int32, (count_, 1), 0) + start_
        return jnp.where(slot_of == slot, 1.0, 0.0).astype(jnp.bfloat16)

    pooled_rows = pick(pool_slot, 2 * POOL)
    key_row = lax.dot_general(
        jnp.broadcast_to(key.astype(jnp.float32), (8, rows)).astype(jnp.bfloat16),
        pooled_rows,
        (((1,), (1,)), ((), ())),
        preferred_element_type=jnp.float32,
    )[0:1, :]
    key_out[...] = jnp.where(most > POOL, FULL, key_row)

    load.wait()
    raw = emb[...]
    norm = jnp.sum(raw * raw, axis=-1, keepdims=True)
    unit[...] = (raw * lax.rsqrt(norm + 1e-06)).astype(jnp.bfloat16)

    def packed(chosen):
        return jnp.dot(chosen, unit[...], preferred_element_type=jnp.float32)

    pool_out[...] = packed(pooled_rows).astype(jnp.bfloat16).reshape(2, POOL, width)

    def remote(src, dst, send, recv, where):
        return pltpu.make_async_remote_copy(
            src_ref=src, dst_ref=dst, send_sem=send, recv_sem=recv, device_id=where, device_id_type=MESH
        )

    def beyond(way):
        return {"dev": 2 * ((mez + (1, nz - 1)[way]) % nz) + mec}

    def hop(s, way):
        return remote(
            pool_out.at[way] if s == 0 else pool.at[s, way, 0],
            pool.at[s + 1, way, 0],
            hop_send.at[s, way],
            hop_recv.at[s + 1, way],
            beyond(way),
        )

    def key_hop(s, way):
        return remote(
            key_out if s == 0 else keys.at[s, way, 0],
            keys.at[s + 1, way, 0],
            key_hop_send.at[s, way],
            key_hop_recv.at[s + 1, way],
            beyond(way),
        )

    def share(s, way):
        return remote(
            pool.at[s, way, 0], pool.at[s, way, 1], share_send.at[s, way], share_recv.at[s, way], {"dev": sibling}
        )

    def key_share(s, way):
        return remote(
            key_out if s == 0 else keys.at[s, way, 0],
            keys.at[s, way, 1],
            key_share_send.at[s, way],
            key_share_recv.at[s, way],
            {"dev": sibling},
        )

    def ways(s):
        return (0, 1) if s < steps else (0,)

    def dispatch(k):
        return remote(
            outgoing.at[k], own.at[owners + k], send_sem.at[k], recv_sem.at[k], {"dev": target(k)}
        )

    def start_dispatch(k, carry):
        dispatch(k).start()
        return carry

    def to_side():
        return remote(side, own.at[1], side_send, side_recv, {"dev": sibling})

    def forward(first_, size, sem, way):
        part = pl.ds(first_, size)
        return remote(
            own.at[part],
            (before if way == 0 else after).at[part],
            pair_send.at[way, sem],
            pair_recv.at[way, sem],
            {"group": (group + (1 if way == 0 else groups - 1)) % groups},
        )

    def tail_piece(s):
        if s == 0:
            return (0, 2, 0)
        return (4 * s - 2, 4 if s < steps else 2, s)

    def base_piece(p):
        return (owners + 2 * p, 2, steps + 1 + p)

    pl.semaphore_wait(barrier, owners + groups - 2)
    for way in (0, 1):
        key_hop(0, way).start()
        hop(0, way).start()
    key_share(0, 0).start()

    in_piece = lax.broadcasted_iota(jnp.int32, (BASE, width), 0).astype(jnp.float32)
    first = lax.broadcasted_iota(jnp.int32, (BASE, width), 1) == 0

    def with_mark(values, k, offset):
        empty = first & (in_piece + offset >= count[k : k + 1, :])
        return jnp.where(empty, DEAD, values).astype(jnp.bfloat16)

    group_of = 8
    for t in range(owners // group_of):
        values = packed(pick(base_slot, group_of * BASE, t * group_of * BASE))
        for c in range(group_of):
            k = t * group_of + c
            piece = with_mark(values[c * BASE : (c + 1) * BASE, :], k, 0.0)
            if k == 0:
                own[owners] = piece
            else:
                outgoing[k] = piece
        if t == 0:
            lax.fori_loop(1, LEAD, start_dispatch, 0)
    values = packed(pick(side_slot, 2 * BASE))
    own[0] = with_mark(values[:BASE, :], 0, float(BASE))
    side[...] = with_mark(values[BASE:, :], 1, float(BASE))
    to_side().start()
    acc[...] = jnp.full_like(acc, -4.0)

    def forward_both(piece):
        forward(*piece, 0).start()
        forward(*piece, 1).start()

    def base_arrives(p, carry):
        def one(k, inner):
            dispatch(k).wait_recv()
            return inner

        lax.fori_loop(2 * p, 2 * p + 2, one, 0)
        forward_both(base_piece(p))
        return carry

    def block(which, found, jb, ib, diagonal=False):
        right = found[pl.ds(jb * per_block, per_block)].reshape(per_block * BASE, width)
        left = own[pl.ds(ib * per_block, per_block)].reshape(per_block * BASE, width)
        scores = lax.dot_general(right, left, (((1,), (1,)), ((), ())), preferred_element_type=jnp.float32)
        drop = right[:, :128].astype(jnp.float32)[:, 0:1] > 1.5
        size = per_block * BASE
        if diagonal:
            drop = drop | (
                (jb == ib)
                & (
                    lax.broadcasted_iota(jnp.int32, (size, size), 0)
                    == lax.broadcasted_iota(jnp.int32, (size, size), 1)
                )
            )
        scores = jnp.where(drop, -1.0, scores)
        best = jnp.max(scores.reshape(size // 8, 8, size), axis=0)
        acc[which, ib] = jnp.maximum(acc[which, ib], best)

    def run(combos, kind, stride_j, start_j, stride_i, start_i):
        across = 2 if stride_i == 2 else blocks

        def body(x, carry):
            jb = stride_j * (x // across) + start_j
            ib = stride_i * (x % across) + start_i
            if kind == "own":
                block(0, own, jb, ib, diagonal=True)
            else:
                block(1, after, jb, ib)
                block(2, before, jb, ib)
            return carry

        lax.fori_loop(0, combos, body, 0)

    wide = lax.broadcasted_iota(jnp.int32, (1, 4 * POOL), 1)
    tall = lax.broadcasted_iota(jnp.int32, (4 * BASE, 1), 0)
    narrow = lax.broadcasted_iota(jnp.int32, (1, 128), 1)

    def select(s):
        parts = []
        for way in ways(s):
            zero, one = keys[s, way, 0], keys[s, way, 1]
            if way == 0:
                parts.append(jnp.where(narrow < POOL, zero, pltpu.roll(one, POOL, 1)))
            else:
                parts.append(jnp.where(narrow < POOL, pltpu.roll(zero, POOL, 1), one))
        n = len(parts)
        held = jnp.concatenate(parts, axis=1)
        lanes, outs = wide[:, : 2 * n * POOL], tall[: 2 * n * BASE, :]
        wanted = (((s - 1) * 2 + (outs // BASE) % 2) * BASE + outs % BASE + 1).astype(jnp.float32)
        match = (lanes // POOL == outs // BASE) & (held == wanted)
        chosen = jnp.where(match, 1.0, 0.0)
        there = pool[s, 0:n].reshape(2 * n * POOL, width)
        values_ = jnp.dot(chosen.astype(jnp.bfloat16), there, preferred_element_type=jnp.float32)
        none = jnp.sum(chosen, axis=1, keepdims=True) < 0.5
        front = lax.broadcasted_iota(jnp.int32, values_.shape, 1) == 0
        values_ = jnp.where(front & none, DEAD, values_).astype(jnp.bfloat16)
        begin, size, _ = tail_piece(s)
        own[begin : begin + size] = values_.reshape(size, BASE, width)

    to_side().wait_recv()
    forward_both(tail_piece(0))
    for s in range(1, steps + 1):
        for way in ways(s):
            hop(s - 1, way).wait_recv()
            key_hop(s - 1, way).wait_recv()
            if s < steps - way:
                key_hop(s, way).start()
                hop(s, way).start()
            key_share(s, way).start()
            share(s, way).start()
        if s < steps:
            per_step = (owners - LEAD + steps - 2) // (steps - 1)
            low = min(LEAD + per_step * (s - 1), owners)
            lax.fori_loop(low, min(low + per_step, owners), start_dispatch, 0)
        if s == 2:
            dispatch(1).wait_recv()
            forward_both(base_piece(0))
        if s > 2:
            lax.fori_loop(2 * s - 5, 2 * s - 3, base_arrives, 0)
        for way in ways(s):
            share(s, way).wait_recv()
            key_share(s, way).wait_recv()
        select(s)
        forward_both(tail_piece(s))
        if s == steps - 2:
            run(4, "own", 2, 0, 2, 0)
    key_share(0, 0).wait_recv()

    worst = jnp.maximum(key_out[...], keys[0, 0, 1])
    for s in range(1, steps + 1):
        for way in ways(s):
            worst = jnp.maximum(worst, jnp.maximum(keys[s, way, 0], keys[s, way, 1]))
    full[0] = worst

    def tell(d):
        return remote(
            full.at[0], full.at[d], full_send.at[d], full_recv.at[d], {"group": (group + d) % groups}
        )

    def start_tell(d, carry):
        tell(d).start()
        return carry

    lax.fori_loop(1, groups, start_tell, 0)

    def pair_arrives(pieces):
        for piece in pieces:
            forward(*piece, 0).wait_recv()
            forward(*piece, 1).wait_recv()

    def base_pair_arrives(p, carry):
        pair_arrives([base_piece(p)])
        return carry

    half = steps // 2
    done = 2 * steps - 3
    lax.fori_loop(done, done + 1, base_arrives, 0)
    pair_arrives([tail_piece(s) for s in range(half + 1)])
    lax.fori_loop(0, half * 2, base_pair_arrives, 0)
    run(4, "pair", 2, 0, 2, 0)
    lax.fori_loop(done + 1, owners // 2, base_arrives, 0)
    run(8, "own", 2, 1, 1, 0)
    run(4, "own", 2, 0, 2, 1)
    run(4, "pair", 2, 0, 2, 1)
    pair_arrives([tail_piece(s) for s in range(half + 1, steps + 1)])
    lax.fori_loop(half * 2, owners // 2, base_pair_arrives, 0)
    run(8, "pair", 2, 1, 1, 0)

    tiles = []
    for which in range(3):
        parts = []
        for b in range(blocks):
            best = jnp.max(acc[which, b], axis=0, keepdims=True)
            parts += [best[:, h * 128 : (h + 1) * 128] for h in range(per_block * BASE // 128)]
        early = jnp.concatenate(parts[len(parts) // 2 :], axis=0)
        late = jnp.concatenate(parts[: len(parts) // 2], axis=0)
        tiles += [early, late]
    spot = lax.broadcasted_iota(jnp.int32, tiles[0].shape, 1) // BASE
    per_tile = 128 // BASE
    for j in range(per_tile):
        mixed = tiles[0] if j == 0 else pltpu.roll(tiles[0], (-BASE * j) % 128, 1)
        for u in range(1, 6):
            moved = tiles[u] if u == j else pltpu.roll(tiles[u], (BASE * (u - j)) % 128, 1)
            mixed = jnp.where(spot >= u, moved, mixed)
        for t in range(owners // per_tile):
            k = per_tile * t + j
            if k == 0:
                got[k] = mixed[t : t + 1, :]
            else:
                ret[k] = mixed[t : t + 1, :]

    def give_back(k):
        return remote(ret.at[k], got.at[k], ret_send.at[k], ret_recv.at[k], {"dev": source(k)})

    def start_back(k, carry):
        give_back(k).start()
        return carry

    lax.fori_loop(1, owners, start_back, 0)

    def drain(k, carry):
        dispatch(k).wait_send()
        return carry

    lax.fori_loop(1, owners, drain, 0)
    to_side().wait_send()
    key_share(0, 0).wait_send()
    for s in range(steps + 1):
        for way in (0, 1):
            if s < steps - way:
                hop(s, way).wait_send()
                key_hop(s, way).wait_send()
        if s > 0:
            for way in ways(s):
                share(s, way).wait_send()
                key_share(s, way).wait_send()
        forward(*tail_piece(s), 0).wait_send()
        forward(*tail_piece(s), 1).wait_send()

    def drain_pair(p, carry):
        forward(*base_piece(p), 0).wait_send()
        forward(*base_piece(p), 1).wait_send()
        return carry

    lax.fori_loop(0, owners // 2, drain_pair, 0)

    def wait_tell(d, carry):
        tell(d).wait()
        return carry

    lax.fori_loop(1, groups, wait_tell, 0)
    flag_ref[...] = jnp.max(full[...], axis=0)

    def wait_back(k, carry):
        give_back(k).wait()
        return carry

    lax.fori_loop(1, owners, wait_back, 0)

    table = got[...].reshape(owners, 128)
    high = table.astype(jnp.bfloat16)
    rest = table - high.astype(jnp.float32)
    middle = rest.astype(jnp.bfloat16)
    low_part = (rest - middle.astype(jnp.float32)).astype(jnp.bfloat16)
    stacked = jnp.concatenate([high, middle, low_part], axis=0)
    picks = jnp.concatenate([hot_b, hot_b, hot_b], axis=0)
    found = lax.dot_general(stacked, picks, (((0,), (0,)), ((), ())), preferred_element_type=jnp.float32)
    mine = lax.broadcasted_iota(jnp.int32, (CAP, 1), 0) == rank
    for which in range(3):
        kept = jnp.where(mine, found[which * CAP : (which + 1) * CAP, :], 0.0)
        line = jnp.sum(kept, axis=0, keepdims=True)
        for a in range(rows // 128):
            out_ref[which, a : a + 1, :] = line[:, a * 128 : (a + 1) * 128]


def all_slots(embeddings, owner):
    owners = lax.axis_size("dev")
    groups = lax.axis_size("group")
    rows, width = embeddings.shape
    vmem = pl.BlockSpec(memory_space=pltpu.VMEM)
    slots = (owners, CAP, width)
    hbm = pl.BlockSpec(memory_space=pltpu.HBM)
    return pl.pallas_call(
        functools.partial(padded, groups=groups, owners=owners),
        out_shape=jax.ShapeDtypeStruct((3, rows // 128, 128), jnp.float32),
        in_specs=[hbm, hbm],
        out_specs=vmem,
        scratch_shapes=[
            pltpu.VMEM((rows, width), jnp.float32),
            pltpu.VMEM((rows // 128, 128), jnp.int32),
            pltpu.VMEM((rows, width), jnp.bfloat16),
            pltpu.VMEM(slots, jnp.bfloat16),
            pltpu.VMEM(slots, jnp.bfloat16),
            pltpu.VMEM(slots, jnp.bfloat16),
            pltpu.VMEM(slots, jnp.bfloat16),
            pltpu.VMEM((3, owners // STAGE, 8, STAGE * CAP), jnp.float32),
            pltpu.VMEM((owners, 1, 128), jnp.float32),
            pltpu.VMEM((owners, 1, 128), jnp.float32),
            pltpu.SemaphoreType.DMA((2,)),
            pltpu.SemaphoreType.DMA((owners,)),
            pltpu.SemaphoreType.DMA((owners,)),
            pltpu.SemaphoreType.DMA((2, owners // PIECE)),
            pltpu.SemaphoreType.DMA((2, owners // PIECE)),
            pltpu.SemaphoreType.DMA((owners,)),
            pltpu.SemaphoreType.DMA((owners,)),
        ],
        compiler_params=pltpu.CompilerParams(
            collective_id=1, has_side_effects=True, vmem_limit_bytes=60 * 1024 * 1024
        ),
    )(embeddings, owner)


def few_slots(embeddings, owner):
    owners = lax.axis_size("dev")
    groups = lax.axis_size("group")
    rows, width = embeddings.shape
    steps = owners // 4
    vmem = pl.BlockSpec(memory_space=pltpu.VMEM)
    hbm = pl.BlockSpec(memory_space=pltpu.HBM)
    entries = (2 * owners, BASE, width)
    size = STAGE * CAP
    pieces = steps + 1 + owners // 2
    ring = pltpu.SemaphoreType.DMA((steps + 1, 2))
    return pl.pallas_call(
        functools.partial(pooled, groups=groups, owners=owners),
        out_shape=(
            jax.ShapeDtypeStruct((3, rows // 128, 128), jnp.float32),
            jax.ShapeDtypeStruct((1, 128), jnp.float32),
        ),
        in_specs=[hbm, hbm],
        out_specs=(vmem, vmem),
        scratch_shapes=[
            pltpu.VMEM((rows, width), jnp.float32),
            pltpu.VMEM((rows // 128, 128), jnp.int32),
            pltpu.VMEM((rows, width), jnp.bfloat16),
            pltpu.VMEM((owners, BASE, width), jnp.bfloat16),
            pltpu.VMEM((BASE, width), jnp.bfloat16),
            pltpu.VMEM(entries, jnp.bfloat16),
            pltpu.VMEM(entries, jnp.bfloat16),
            pltpu.VMEM(entries, jnp.bfloat16),
            pltpu.VMEM((3, 2 * owners * BASE // size, 8, size), jnp.float32),
            pltpu.VMEM((owners, 1, 128), jnp.float32),
            pltpu.VMEM((owners, 1, 128), jnp.float32),
            pltpu.VMEM((2, POOL, width), jnp.bfloat16),
            pltpu.VMEM((steps + 1, 2, 2, POOL, width), jnp.bfloat16),
            pltpu.VMEM((1, 128), jnp.float32),
            pltpu.VMEM((steps + 1, 2, 2, 1, 128), jnp.float32),
            pltpu.VMEM((groups, 1, 128), jnp.float32),
            pltpu.SemaphoreType.DMA((2,)),
            pltpu.SemaphoreType.DMA((owners,)),
            pltpu.SemaphoreType.DMA((owners,)),
            pltpu.SemaphoreType.DMA((2, pieces)),
            pltpu.SemaphoreType.DMA((2, pieces)),
            pltpu.SemaphoreType.DMA((owners,)),
            pltpu.SemaphoreType.DMA((owners,)),
            ring,
            ring,
            ring,
            ring,
            ring,
            ring,
            ring,
            ring,
            pltpu.SemaphoreType.DMA((groups,)),
            pltpu.SemaphoreType.DMA((groups,)),
            pltpu.SemaphoreType.DMA,
            pltpu.SemaphoreType.DMA,
        ],
        compiler_params=pltpu.CompilerParams(
            collective_id=0, has_side_effects=True, vmem_limit_bytes=60 * 1024 * 1024
        ),
    )(embeddings, owner)


def local(embeddings, owner):
    rows = embeddings.shape[0]
    lines = owner.reshape(rows // 128, 128)
    out, flag = few_slots(embeddings, lines)
    out = lax.cond(jnp.max(flag) > FULL / 2, lambda e, o, kept: all_slots(e, o), lambda e, o, kept: kept, embeddings, lines, out)
    return tuple(out[which].reshape(rows) for which in range(3))


def solution(mesh):
    placed = (P(("group", "dev"), None), P(("group", "dev")))
    return jax.shard_map(
        local,
        mesh=mesh,
        in_specs=placed,
        out_specs=(P(("group", "dev")), P(("group", "dev")), P(("group", "dev"))),
        check_vma=False,
    )
```

```python
import functools

import jax
import jax.numpy as jnp
from jax import lax
from jax.experimental import pallas as pl
from jax.experimental.pallas import tpu as pltpu
from jax.sharding import PartitionSpec as P

CAP = 32
DEAD = 2.0
STAGE = 8
PIECE = 1
PACK = 4
BASE = 16
POOL = 64
FULL = 1000.0
LEAD = 8
MESH = pl.DeviceIdType.MESH


def room(step):
    return 64 if step <= 3 else 48 if step <= 6 else 32


def ring_offset(k, nz):
    j = k // 2
    size = (j + 1) // 2
    return jnp.where(j % 2 == 1, size, -size)


def padded(
    emb_hbm,
    owner_hbm,
    out_ref,
    emb,
    owner_ref,
    unit,
    outgoing,
    own,
    before,
    after,
    acc,
    ret,
    got,
    load_sem,
    send_sem,
    recv_sem,
    pair_send,
    pair_recv,
    ret_send,
    ret_recv,
    *,
    groups,
    owners,
):
    rows, width = emb.shape
    nz = owners // 2
    group = lax.axis_index("group")
    me = lax.axis_index("dev")
    mez, mec = me // 2, me % 2
    stages = owners // STAGE
    here = 0

    load_owner = pltpu.make_async_copy(owner_hbm, owner_ref, load_sem.at[0])
    load_owner.start()
    load = pltpu.make_async_copy(emb_hbm, emb, load_sem.at[1])
    load.start()

    def target(k):
        z = (mez + ring_offset(k, nz) + nz) % nz
        return 2 * z + (mec + k) % 2

    def source(k):
        z = (mez - ring_offset(k, nz) + nz) % nz
        return 2 * z + (mec + k) % 2

    barrier = pltpu.get_barrier_semaphore()

    def greet(d, carry):
        pl.semaphore_signal(barrier, inc=1, device_id={"dev": (me + d) % owners}, device_id_type=MESH)
        return carry

    lax.fori_loop(1, owners, greet, 0)
    later = (group + 1) % groups
    earlier = (group + groups - 1) % groups
    pl.semaphore_signal(barrier, inc=1, device_id={"group": later}, device_id_type=MESH)
    pl.semaphore_signal(barrier, inc=1, device_id={"group": earlier}, device_id_type=MESH)

    load_owner.wait()

    owner = jnp.concatenate([owner_ref[a : a + 1, :] for a in range(rows // 128)], axis=1)
    chunk = lax.broadcasted_iota(jnp.int32, (owners, 1), 0)
    cluster = 2 * ((mez + ring_offset(chunk, nz) + nz) % nz) + (mec + chunk) % 2
    hot = owner == cluster
    hot_f = jnp.where(hot, 1.0, 0.0)
    hot_b = hot_f.astype(jnp.bfloat16)
    earlier_row = lax.broadcasted_iota(jnp.int32, (rows, rows), 0) < lax.broadcasted_iota(
        jnp.int32, (rows, rows), 1
    )
    ahead = jnp.dot(
        hot_b, jnp.where(earlier_row, 1.0, 0.0).astype(jnp.bfloat16), preferred_element_type=jnp.float32
    )
    rank = jnp.sum(ahead * hot_f, axis=0, keepdims=True).astype(jnp.int32)
    chunk_of = jnp.sum(hot_f * chunk.astype(jnp.float32), axis=0, keepdims=True).astype(jnp.int32)
    slot_of = chunk_of * CAP + rank
    count = jnp.sum(hot_f, axis=1, keepdims=True)

    load.wait()
    raw = emb[...]
    norm = jnp.sum(raw * raw, axis=-1, keepdims=True)
    unit[...] = (raw * lax.rsqrt(norm + 1e-06)).astype(jnp.bfloat16)

    def dispatch(k):
        return pltpu.make_async_remote_copy(
            src_ref=outgoing.at[k],
            dst_ref=own.at[k],
            send_sem=send_sem.at[k],
            recv_sem=recv_sem.at[k],
            device_id={"dev": target(k)},
            device_id_type=MESH,
        )

    def start_dispatch(k, carry):
        dispatch(k).start()
        return carry

    slot = lax.broadcasted_iota(jnp.int32, (PACK * CAP, 1), 0)
    first = lax.broadcasted_iota(jnp.int32, (CAP, width), 1) == 0
    in_chunk = lax.broadcasted_iota(jnp.int32, (CAP, width), 0).astype(jnp.float32)
    for t in range(owners // PACK):
        pick = jnp.where(slot_of == slot + t * PACK * CAP, 1.0, 0.0).astype(jnp.bfloat16)
        packed = jnp.dot(pick, unit[...], preferred_element_type=jnp.float32)
        for c in range(PACK):
            k = t * PACK + c
            empty = first & (in_chunk >= count[k : k + 1, :])
            piece = jnp.where(empty, DEAD, packed[c * CAP : (c + 1) * CAP, :]).astype(jnp.bfloat16)
            if k == here:
                own[k] = piece
            else:
                outgoing[k] = piece
        if t == 0:
            pl.semaphore_wait(barrier, owners + 1)
        lax.fori_loop(max(t * PACK, 1), (t + 1) * PACK, start_dispatch, 0)

    acc[...] = jnp.full_like(acc, -4.0)

    def forward(p, way):
        part = pl.ds(p * PIECE, PIECE)
        return pltpu.make_async_remote_copy(
            src_ref=own.at[part],
            dst_ref=(before if way == 0 else after).at[part],
            send_sem=pair_send.at[way, p],
            recv_sem=pair_recv.at[way, p],
            device_id={"group": later if way == 0 else earlier},
            device_id_type=MESH,
        )

    def block(which, found, jb, ib, diagonal=False):
        right = found[pl.ds(jb * STAGE, STAGE)].reshape(STAGE * CAP, width)
        left = own[pl.ds(ib * STAGE, STAGE)].reshape(STAGE * CAP, width)
        scores = lax.dot_general(right, left, (((1,), (1,)), ((), ())), preferred_element_type=jnp.float32)
        drop = right[:, :128].astype(jnp.float32)[:, 0:1] > 1.5
        if diagonal:
            size = STAGE * CAP
            drop = drop | (
                lax.broadcasted_iota(jnp.int32, (size, size), 0) == lax.broadcasted_iota(jnp.int32, (size, size), 1)
            )
        scores = jnp.where(drop, -1.0, scores)
        best = jnp.max(scores.reshape(STAGE * CAP // 8, 8, STAGE * CAP), axis=0)
        acc[which, ib] = jnp.maximum(acc[which, ib], best)

    def arrive(t):
        def chunk_arrives(k, carry):
            dispatch(k).wait_recv()
            return carry

        def piece_arrives(p, carry):
            lax.fori_loop(p * PIECE, (p + 1) * PIECE, chunk_arrives, 0)
            forward(p, 0).start()
            forward(p, 1).start()
            return carry

        per = STAGE // PIECE
        if t == 0:
            lax.fori_loop(1, PIECE, chunk_arrives, 0)
            forward(0, 0).start()
            forward(0, 1).start()
            lax.fori_loop(1, per, piece_arrives, 0)
        else:
            lax.fori_loop(t * per, (t + 1) * per, piece_arrives, 0)

    def pair_arrives(t):
        def piece(p, carry):
            forward(p, 0).wait_recv()
            forward(p, 1).wait_recv()
            return carry

        per = STAGE // PIECE
        lax.fori_loop(t * per, (t + 1) * per, piece, 0)

    def both(jb, ib):
        block(1, after, jb, ib)
        block(2, before, jb, ib)

    for t in range(stages):
        arrive(t)
        block(0, own, t, t, diagonal=True)

        def own_blocks(b, carry, t=t):
            block(0, own, t, b)
            block(0, own, b, t)
            return carry

        lax.fori_loop(0, t, own_blocks, 0)
        if t > 0:
            pair_arrives(t - 1)

            def new_rows(b, carry, t=t):
                both(b, t)
                return carry

            def new_found(b, carry, t=t):
                both(t - 1, b)
                return carry

            lax.fori_loop(0, t, new_rows, 0)
            lax.fori_loop(0, t, new_found, 0)
    pair_arrives(stages - 1)

    def last_found(b, carry):
        both(stages - 1, b)
        return carry

    lax.fori_loop(0, stages, last_found, 0)

    tiles = []
    for which in range(3):
        parts = []
        for b in range(stages):
            best = jnp.max(acc[which, b], axis=0, keepdims=True)
            parts += [best[:, h * 128 : (h + 1) * 128] for h in range(STAGE * CAP // 128)]
        tiles.append(jnp.concatenate(parts, axis=0))
    lane = lax.broadcasted_iota(jnp.int32, tiles[0].shape, 1)
    per_tile = 128 // CAP
    for j in range(per_tile):
        moved = [pltpu.roll(tiles[w], (CAP * (w - j)) % 128, 1) if (w - j) % 4 else tiles[w] for w in range(3)]
        mixed = jnp.where(lane < CAP, moved[0], jnp.where(lane < 2 * CAP, moved[1], moved[2]))
        for t in range(owners // per_tile):
            k = per_tile * t + j
            if k == here:
                got[k] = mixed[t : t + 1, :]
            else:
                ret[k] = mixed[t : t + 1, :]

    def give_back(k):
        return pltpu.make_async_remote_copy(
            src_ref=ret.at[k],
            dst_ref=got.at[k],
            send_sem=ret_send.at[k],
            recv_sem=ret_recv.at[k],
            device_id={"dev": source(k)},
            device_id_type=MESH,
        )

    def start_back(k, carry):
        give_back(k).start()
        return carry

    lax.fori_loop(1, owners, start_back, 0)

    def drain(k, carry):
        dispatch(k).wait_send()
        return carry

    lax.fori_loop(1, owners, drain, 0)

    def drain_pair(p, carry):
        forward(p, 0).wait_send()
        forward(p, 1).wait_send()
        return carry

    lax.fori_loop(0, owners // PIECE, drain_pair, 0)

    def wait_back(k, carry):
        give_back(k).wait()
        return carry

    lax.fori_loop(1, owners, wait_back, 0)

    table = got[...].reshape(owners, 128)
    high = table.astype(jnp.bfloat16)
    rest = table - high.astype(jnp.float32)
    middle = rest.astype(jnp.bfloat16)
    low = (rest - middle.astype(jnp.float32)).astype(jnp.bfloat16)
    stacked = jnp.concatenate([high, middle, low], axis=0)
    picks = jnp.concatenate([hot_b, hot_b, hot_b], axis=0)
    found = lax.dot_general(stacked, picks, (((0,), (0,)), ((), ())), preferred_element_type=jnp.float32)
    mine = lax.broadcasted_iota(jnp.int32, (CAP, 1), 0) == rank
    for which in range(3):
        kept = jnp.where(mine, found[which * CAP : (which + 1) * CAP, :], 0.0)
        line = jnp.sum(kept, axis=0, keepdims=True)
        for a in range(rows // 128):
            out_ref[which, a : a + 1, :] = line[:, a * 128 : (a + 1) * 128]


def pooled(
    emb_hbm,
    owner_hbm,
    out_ref,
    flag_ref,
    emb,
    owner_ref,
    unit,
    outgoing,
    side,
    own,
    before,
    after,
    acc,
    ret,
    got,
    pool_out,
    pool,
    key_out,
    keys,
    full,
    load_sem,
    send_sem,
    recv_sem,
    pair_send,
    pair_recv,
    ret_send,
    ret_recv,
    hop_send,
    hop_recv,
    share_send,
    share_recv,
    key_hop_send,
    key_hop_recv,
    key_share_send,
    key_share_recv,
    full_send,
    full_recv,
    side_send,
    side_recv,
    *,
    groups,
    owners,
):
    rows, width = emb.shape
    nz = owners // 2
    group = lax.axis_index("group")
    me = lax.axis_index("dev")
    mez, mec = me // 2, me % 2
    sibling = 2 * mez + 1 - mec
    steps = nz // 2
    per_block = STAGE * CAP // BASE
    blocks = 2 * owners // per_block

    load_owner = pltpu.make_async_copy(owner_hbm, owner_ref, load_sem.at[0])
    load_owner.start()
    load = pltpu.make_async_copy(emb_hbm, emb, load_sem.at[1])
    load.start()

    def target(k):
        return 2 * ((mez + ring_offset(k, nz) + nz) % nz) + (mec + k) % 2

    def source(k):
        return 2 * ((mez - ring_offset(k, nz) + nz) % nz) + (mec + k) % 2

    barrier = pltpu.get_barrier_semaphore()

    def greet(d, carry):
        pl.semaphore_signal(barrier, inc=1, device_id={"dev": (me + d) % owners}, device_id_type=MESH)
        return carry

    def greet_group(d, carry):
        pl.semaphore_signal(barrier, inc=1, device_id={"group": (group + d) % groups}, device_id_type=MESH)
        return carry

    lax.fori_loop(1, owners, greet, 0)
    lax.fori_loop(1, groups, greet_group, 0)

    load_owner.wait()
    owner = jnp.concatenate([owner_ref[a : a + 1, :] for a in range(rows // 128)], axis=1)
    chunk = lax.broadcasted_iota(jnp.int32, (owners, 1), 0)
    cluster = 2 * ((mez + ring_offset(chunk, nz) + nz) % nz) + (mec + chunk) % 2
    hot_f = jnp.where(owner == cluster, 1.0, 0.0)
    hot_b = hot_f.astype(jnp.bfloat16)
    earlier_row = lax.broadcasted_iota(jnp.int32, (rows, rows), 0) < lax.broadcasted_iota(
        jnp.int32, (rows, rows), 1
    )
    ahead = jnp.dot(
        hot_b, jnp.where(earlier_row, 1.0, 0.0).astype(jnp.bfloat16), preferred_element_type=jnp.float32
    )

    def of_row(per_chunk):
        return jnp.sum(hot_f * per_chunk, axis=0, keepdims=True).astype(jnp.int32)

    rank = of_row(ahead)
    chunk_of = of_row(chunk.astype(jnp.float32))
    count = jnp.sum(hot_f, axis=1, keepdims=True)
    counts = lax.dot_general(
        jnp.ones((8, rows), jnp.bfloat16), hot_b, (((1,), (1,)), ((), ())), preferred_element_type=jnp.float32
    )[0:1, :]

    lane = lax.broadcasted_iota(jnp.int32, (1, owners), 1)
    spill = jnp.where(lane >= 2, jnp.maximum(counts - BASE, 0.0), 0.0)

    def way_of(k):
        return 1 - (k // 2) % 2

    same_way = way_of(lane) == way_of(chunk)
    start = jnp.sum(jnp.where(same_way & (lane > chunk), spill, 0.0), axis=1, keepdims=True)
    filled = jnp.sum(jnp.where(same_way & (lane >= chunk), spill, 0.0), axis=1, keepdims=True)
    step_of = (chunk // 2 + 1) // 2
    space = jnp.full((owners, 1), float(room(1)), jnp.float32)
    for s in range(2, steps + 1):
        space = jnp.where(step_of >= s, float(room(s)), space)
    excess = jnp.max(jnp.where(chunk >= 2, filled - space, -1.0), axis=0, keepdims=True)
    at = of_row(start) + rank - BASE
    spilled = (rank >= BASE) & (chunk_of >= 2) & (at < POOL)
    pool_slot = jnp.where(spilled, way_of(chunk_of) * POOL + at, -1)
    hops = (chunk_of // 2 + 1) // 2
    key = jnp.where(spilled, ((hops - 1) * 2 + chunk_of % 2) * BASE + rank - BASE + 1, 0)
    base_slot = jnp.where(rank < BASE, chunk_of * BASE + rank, -1)
    side_slot = jnp.where((rank >= BASE) & (chunk_of < 2), chunk_of * BASE + rank - BASE, -1)

    def pick(slot_of, count_, start_=0):
        slot = lax.broadcasted_iota(jnp.int32, (count_, 1), 0) + start_
        return jnp.where(slot_of == slot, 1.0, 0.0).astype(jnp.bfloat16)

    pooled_rows = pick(pool_slot, 2 * POOL)
    key_row = lax.dot_general(
        jnp.broadcast_to(key.astype(jnp.float32), (8, rows)).astype(jnp.bfloat16),
        pooled_rows,
        (((1,), (1,)), ((), ())),
        preferred_element_type=jnp.float32,
    )[0:1, :]
    key_out[...] = jnp.where(excess > 0.0, FULL, key_row)

    load.wait()
    raw = emb[...]
    norm = jnp.sum(raw * raw, axis=-1, keepdims=True)
    unit[...] = (raw * lax.rsqrt(norm + 1e-06)).astype(jnp.bfloat16)

    def packed(chosen):
        return jnp.dot(chosen, unit[...], preferred_element_type=jnp.float32)

    pool_out[...] = packed(pooled_rows).astype(jnp.bfloat16).reshape(2, POOL, width)

    def remote(src, dst, send, recv, where):
        return pltpu.make_async_remote_copy(
            src_ref=src, dst_ref=dst, send_sem=send, recv_sem=recv, device_id=where, device_id_type=MESH
        )

    def beyond(way):
        return {"dev": 2 * ((mez + (1, nz - 1)[way]) % nz) + mec}

    def hop(s, way):
        part = pl.ds(0, room(s + 1))
        return remote(
            pool_out.at[way, part] if s == 0 else pool.at[s, way, 0, part],
            pool.at[s + 1, way, 0, part],
            hop_send.at[s, way],
            hop_recv.at[s + 1, way],
            beyond(way),
        )

    def key_hop(s, way):
        return remote(
            key_out if s == 0 else keys.at[s, way, 0],
            keys.at[s + 1, way, 0],
            key_hop_send.at[s, way],
            key_hop_recv.at[s + 1, way],
            beyond(way),
        )

    def share(s, way):
        part = pl.ds(0, room(s))
        return remote(
            pool.at[s, way, 0, part],
            pool.at[s, way, 1, part],
            share_send.at[s, way],
            share_recv.at[s, way],
            {"dev": sibling},
        )

    def key_share(s, way):
        return remote(
            key_out if s == 0 else keys.at[s, way, 0],
            keys.at[s, way, 1],
            key_share_send.at[s, way],
            key_share_recv.at[s, way],
            {"dev": sibling},
        )

    def ways(s):
        return (0, 1) if s < steps else (0,)

    def dispatch(k):
        return remote(
            outgoing.at[k], own.at[owners + k], send_sem.at[k], recv_sem.at[k], {"dev": target(k)}
        )

    def start_dispatch(k, carry):
        dispatch(k).start()
        return carry

    def to_side():
        return remote(side, own.at[1], side_send, side_recv, {"dev": sibling})

    def forward(first_, size, sem, way):
        part = pl.ds(first_, size)
        return remote(
            own.at[part],
            (before if way == 0 else after).at[part],
            pair_send.at[way, sem],
            pair_recv.at[way, sem],
            {"group": (group + (1 if way == 0 else groups - 1)) % groups},
        )

    def tail_piece(s):
        if s == 0:
            return (0, 2, 0)
        return (4 * s - 2, 4 if s < steps else 2, s)

    def base_piece(p):
        return (owners + 2 * p, 2, steps + 1 + p)

    pl.semaphore_wait(barrier, owners + groups - 2)
    for way in (0, 1):
        key_hop(0, way).start()
        hop(0, way).start()
    key_share(0, 0).start()

    in_piece = lax.broadcasted_iota(jnp.int32, (BASE, width), 0).astype(jnp.float32)
    first = lax.broadcasted_iota(jnp.int32, (BASE, width), 1) == 0

    def with_mark(values, k, offset):
        empty = first & (in_piece + offset >= count[k : k + 1, :])
        return jnp.where(empty, DEAD, values).astype(jnp.bfloat16)

    group_of = 8
    for t in range(owners // group_of):
        values = packed(pick(base_slot, group_of * BASE, t * group_of * BASE))
        for c in range(group_of):
            k = t * group_of + c
            piece = with_mark(values[c * BASE : (c + 1) * BASE, :], k, 0.0)
            if k == 0:
                own[owners] = piece
            else:
                outgoing[k] = piece
        if t == 0:
            lax.fori_loop(1, LEAD, start_dispatch, 0)
    values = packed(pick(side_slot, 2 * BASE))
    own[0] = with_mark(values[:BASE, :], 0, float(BASE))
    side[...] = with_mark(values[BASE:, :], 1, float(BASE))
    to_side().start()
    acc[...] = jnp.full_like(acc, -4.0)
    for s in range(1, steps + 1):
        if room(s) < POOL:
            for way in ways(s):
                for core in (0, 1):
                    pool[s, way, core, room(s) :] = jnp.zeros((POOL - room(s), width), jnp.bfloat16)

    def forward_both(piece):
        forward(*piece, 0).start()
        forward(*piece, 1).start()

    def base_arrives(p, carry):
        def one(k, inner):
            dispatch(k).wait_recv()
            return inner

        lax.fori_loop(2 * p, 2 * p + 2, one, 0)
        forward_both(base_piece(p))
        return carry

    def block(which, found, jb, ib, diagonal=False):
        right = found[pl.ds(jb * per_block, per_block)].reshape(per_block * BASE, width)
        left = own[pl.ds(ib * per_block, per_block)].reshape(per_block * BASE, width)
        scores = lax.dot_general(right, left, (((1,), (1,)), ((), ())), preferred_element_type=jnp.float32)
        drop = right[:, :128].astype(jnp.float32)[:, 0:1] > 1.5
        size = per_block * BASE
        if diagonal:
            drop = drop | (
                (jb == ib)
                & (
                    lax.broadcasted_iota(jnp.int32, (size, size), 0)
                    == lax.broadcasted_iota(jnp.int32, (size, size), 1)
                )
            )
        scores = jnp.where(drop, -1.0, scores)
        best = jnp.max(scores.reshape(size // 8, 8, size), axis=0)
        acc[which, ib] = jnp.maximum(acc[which, ib], best)

    def run(combos, kind, stride_j, start_j, stride_i, start_i):
        across = 2 if stride_i == 2 else blocks

        def body(x, carry):
            jb = stride_j * (x // across) + start_j
            ib = stride_i * (x % across) + start_i
            if kind == "own":
                block(0, own, jb, ib, diagonal=True)
            else:
                block(1, after, jb, ib)
                block(2, before, jb, ib)
            return carry

        lax.fori_loop(0, combos, body, 0)

    wide = lax.broadcasted_iota(jnp.int32, (1, 4 * POOL), 1)
    tall = lax.broadcasted_iota(jnp.int32, (4 * BASE, 1), 0)
    narrow = lax.broadcasted_iota(jnp.int32, (1, 128), 1)

    def select(s):
        parts = []
        for way in ways(s):
            zero, one = keys[s, way, 0], keys[s, way, 1]
            if way == 0:
                parts.append(jnp.where(narrow < POOL, zero, pltpu.roll(one, POOL, 1)))
            else:
                parts.append(jnp.where(narrow < POOL, pltpu.roll(zero, POOL, 1), one))
        n = len(parts)
        held = jnp.concatenate(parts, axis=1)
        lanes, outs = wide[:, : 2 * n * POOL], tall[: 2 * n * BASE, :]
        wanted = (((s - 1) * 2 + (outs // BASE) % 2) * BASE + outs % BASE + 1).astype(jnp.float32)
        match = (lanes // POOL == outs // BASE) & (held == wanted)
        chosen = jnp.where(match, 1.0, 0.0)
        there = pool[s, 0:n].reshape(2 * n * POOL, width)
        values_ = jnp.dot(chosen.astype(jnp.bfloat16), there, preferred_element_type=jnp.float32)
        none = jnp.sum(chosen, axis=1, keepdims=True) < 0.5
        front = lax.broadcasted_iota(jnp.int32, values_.shape, 1) == 0
        values_ = jnp.where(front & none, DEAD, values_).astype(jnp.bfloat16)
        begin, size, _ = tail_piece(s)
        own[begin : begin + size] = values_.reshape(size, BASE, width)

    to_side().wait_recv()
    forward_both(tail_piece(0))
    for s in range(1, steps + 1):
        for way in ways(s):
            hop(s - 1, way).wait_recv()
            key_hop(s - 1, way).wait_recv()
            if s < steps - way:
                key_hop(s, way).start()
                hop(s, way).start()
            key_share(s, way).start()
            share(s, way).start()
        if s < steps:
            per_step = (owners - LEAD + steps - 2) // (steps - 1)
            low = min(LEAD + per_step * (s - 1), owners)
            lax.fori_loop(low, min(low + per_step, owners), start_dispatch, 0)
        for way in ways(s):
            share(s, way).wait_recv()
            key_share(s, way).wait_recv()
        select(s)
        forward_both(tail_piece(s))
        if s == 2:
            dispatch(1).wait_recv()
            forward_both(base_piece(0))
        if s > 2:
            lax.fori_loop(2 * s - 5, 2 * s - 3, base_arrives, 0)
        if s == steps - 2:
            run(4, "own", 2, 0, 2, 0)
    key_share(0, 0).wait_recv()

    worst = jnp.maximum(key_out[...], keys[0, 0, 1])
    for s in range(1, steps + 1):
        for way in ways(s):
            worst = jnp.maximum(worst, jnp.maximum(keys[s, way, 0], keys[s, way, 1]))
    full[0] = worst

    def tell(d):
        return remote(
            full.at[0], full.at[d], full_send.at[d], full_recv.at[d], {"group": (group + d) % groups}
        )

    def start_tell(d, carry):
        tell(d).start()
        return carry

    lax.fori_loop(1, groups, start_tell, 0)

    def pair_arrives(pieces):
        for piece in pieces:
            forward(*piece, 0).wait_recv()
            forward(*piece, 1).wait_recv()

    def base_pair_arrives(p, carry):
        pair_arrives([base_piece(p)])
        return carry

    half = steps // 2
    done = 2 * steps - 3
    lax.fori_loop(done, done + 1, base_arrives, 0)
    pair_arrives([tail_piece(s) for s in range(half + 1)])
    lax.fori_loop(0, half * 2, base_pair_arrives, 0)
    run(4, "pair", 2, 0, 2, 0)
    lax.fori_loop(done + 1, owners // 2, base_arrives, 0)
    run(8, "own", 2, 1, 1, 0)
    run(4, "own", 2, 0, 2, 1)
    run(4, "pair", 2, 0, 2, 1)
    pair_arrives([tail_piece(s) for s in range(half + 1, steps + 1)])
    run(4, "pair", 0, 1, 1, 0)
    lax.fori_loop(half * 2, owners // 2, base_pair_arrives, 0)
    run(4, "pair", 0, 3, 1, 0)

    tiles = []
    for which in range(3):
        parts = []
        for b in range(blocks):
            best = jnp.max(acc[which, b], axis=0, keepdims=True)
            parts += [best[:, h * 128 : (h + 1) * 128] for h in range(per_block * BASE // 128)]
        early = jnp.concatenate(parts[len(parts) // 2 :], axis=0)
        late = jnp.concatenate(parts[: len(parts) // 2], axis=0)
        tiles += [early, late]
    spot = lax.broadcasted_iota(jnp.int32, tiles[0].shape, 1) // BASE
    per_tile = 128 // BASE
    for j in range(per_tile):
        mixed = tiles[0] if j == 0 else pltpu.roll(tiles[0], (-BASE * j) % 128, 1)
        for u in range(1, 6):
            moved = tiles[u] if u == j else pltpu.roll(tiles[u], (BASE * (u - j)) % 128, 1)
            mixed = jnp.where(spot >= u, moved, mixed)
        for t in range(owners // per_tile):
            k = per_tile * t + j
            if k == 0:
                got[k] = mixed[t : t + 1, :]
            else:
                ret[k] = mixed[t : t + 1, :]

    def give_back(k):
        return remote(ret.at[k], got.at[k], ret_send.at[k], ret_recv.at[k], {"dev": source(k)})

    def start_back(k, carry):
        give_back(owners - k).start()
        return carry

    lax.fori_loop(1, owners, start_back, 0)

    def drain(k, carry):
        dispatch(k).wait_send()
        return carry

    lax.fori_loop(1, owners, drain, 0)
    to_side().wait_send()
    key_share(0, 0).wait_send()
    for s in range(steps + 1):
        for way in (0, 1):
            if s < steps - way:
                hop(s, way).wait_send()
                key_hop(s, way).wait_send()
        if s > 0:
            for way in ways(s):
                share(s, way).wait_send()
                key_share(s, way).wait_send()
        forward(*tail_piece(s), 0).wait_send()
        forward(*tail_piece(s), 1).wait_send()

    def drain_pair(p, carry):
        forward(*base_piece(p), 0).wait_send()
        forward(*base_piece(p), 1).wait_send()
        return carry

    lax.fori_loop(0, owners // 2, drain_pair, 0)

    def wait_tell(d, carry):
        tell(d).wait()
        return carry

    lax.fori_loop(1, groups, wait_tell, 0)
    flag_ref[0, 0] = jnp.max(full[...])

    def wait_back(k, carry):
        give_back(k).wait()
        return carry

    lax.fori_loop(1, owners, wait_back, 0)

    table = got[...].reshape(owners, 128)
    high = table.astype(jnp.bfloat16)
    rest = table - high.astype(jnp.float32)
    middle = rest.astype(jnp.bfloat16)
    low_part = (rest - middle.astype(jnp.float32)).astype(jnp.bfloat16)
    stacked = jnp.concatenate([high, middle, low_part], axis=0)
    picks = jnp.concatenate([hot_b, hot_b, hot_b], axis=0)
    found = lax.dot_general(stacked, picks, (((0,), (0,)), ((), ())), preferred_element_type=jnp.float32)
    mine = lax.broadcasted_iota(jnp.int32, (CAP, 1), 0) == rank
    for which in range(3):
        kept = jnp.where(mine, found[which * CAP : (which + 1) * CAP, :], 0.0)
        line = jnp.sum(kept, axis=0, keepdims=True)
        for a in range(rows // 128):
            out_ref[which, a : a + 1, :] = line[:, a * 128 : (a + 1) * 128]


def all_slots(embeddings, owner):
    owners = lax.axis_size("dev")
    groups = lax.axis_size("group")
    rows, width = embeddings.shape
    vmem = pl.BlockSpec(memory_space=pltpu.VMEM)
    slots = (owners, CAP, width)
    hbm = pl.BlockSpec(memory_space=pltpu.HBM)
    return pl.pallas_call(
        functools.partial(padded, groups=groups, owners=owners),
        out_shape=jax.ShapeDtypeStruct((3, rows // 128, 128), jnp.float32),
        in_specs=[hbm, hbm],
        out_specs=vmem,
        scratch_shapes=[
            pltpu.VMEM((rows, width), jnp.float32),
            pltpu.VMEM((rows // 128, 128), jnp.int32),
            pltpu.VMEM((rows, width), jnp.bfloat16),
            pltpu.VMEM(slots, jnp.bfloat16),
            pltpu.VMEM(slots, jnp.bfloat16),
            pltpu.VMEM(slots, jnp.bfloat16),
            pltpu.VMEM(slots, jnp.bfloat16),
            pltpu.VMEM((3, owners // STAGE, 8, STAGE * CAP), jnp.float32),
            pltpu.VMEM((owners, 1, 128), jnp.float32),
            pltpu.VMEM((owners, 1, 128), jnp.float32),
            pltpu.SemaphoreType.DMA((2,)),
            pltpu.SemaphoreType.DMA((owners,)),
            pltpu.SemaphoreType.DMA((owners,)),
            pltpu.SemaphoreType.DMA((2, owners // PIECE)),
            pltpu.SemaphoreType.DMA((2, owners // PIECE)),
            pltpu.SemaphoreType.DMA((owners,)),
            pltpu.SemaphoreType.DMA((owners,)),
        ],
        compiler_params=pltpu.CompilerParams(
            collective_id=1, has_side_effects=True, vmem_limit_bytes=60 * 1024 * 1024
        ),
    )(embeddings, owner)


def few_slots(embeddings, owner):
    owners = lax.axis_size("dev")
    groups = lax.axis_size("group")
    rows, width = embeddings.shape
    steps = owners // 4
    vmem = pl.BlockSpec(memory_space=pltpu.VMEM)
    hbm = pl.BlockSpec(memory_space=pltpu.HBM)
    entries = (2 * owners, BASE, width)
    size = STAGE * CAP
    pieces = steps + 1 + owners // 2
    ring = pltpu.SemaphoreType.DMA((steps + 1, 2))
    return pl.pallas_call(
        functools.partial(pooled, groups=groups, owners=owners),
        out_shape=(
            jax.ShapeDtypeStruct((3, rows // 128, 128), jnp.float32),
            jax.ShapeDtypeStruct((1, 1), jnp.float32),
        ),
        in_specs=[hbm, hbm],
        out_specs=(vmem, pl.BlockSpec(memory_space=pltpu.SMEM)),
        scratch_shapes=[
            pltpu.VMEM((rows, width), jnp.float32),
            pltpu.VMEM((rows // 128, 128), jnp.int32),
            pltpu.VMEM((rows, width), jnp.bfloat16),
            pltpu.VMEM((owners, BASE, width), jnp.bfloat16),
            pltpu.VMEM((BASE, width), jnp.bfloat16),
            pltpu.VMEM(entries, jnp.bfloat16),
            pltpu.VMEM(entries, jnp.bfloat16),
            pltpu.VMEM(entries, jnp.bfloat16),
            pltpu.VMEM((3, 2 * owners * BASE // size, 8, size), jnp.float32),
            pltpu.VMEM((owners, 1, 128), jnp.float32),
            pltpu.VMEM((owners, 1, 128), jnp.float32),
            pltpu.VMEM((2, POOL, width), jnp.bfloat16),
            pltpu.VMEM((steps + 1, 2, 2, POOL, width), jnp.bfloat16),
            pltpu.VMEM((1, 128), jnp.float32),
            pltpu.VMEM((steps + 1, 2, 2, 1, 128), jnp.float32),
            pltpu.VMEM((groups, 1, 128), jnp.float32),
            pltpu.SemaphoreType.DMA((2,)),
            pltpu.SemaphoreType.DMA((owners,)),
            pltpu.SemaphoreType.DMA((owners,)),
            pltpu.SemaphoreType.DMA((2, pieces)),
            pltpu.SemaphoreType.DMA((2, pieces)),
            pltpu.SemaphoreType.DMA((owners,)),
            pltpu.SemaphoreType.DMA((owners,)),
            ring,
            ring,
            ring,
            ring,
            ring,
            ring,
            ring,
            ring,
            pltpu.SemaphoreType.DMA((groups,)),
            pltpu.SemaphoreType.DMA((groups,)),
            pltpu.SemaphoreType.DMA,
            pltpu.SemaphoreType.DMA,
        ],
        compiler_params=pltpu.CompilerParams(
            collective_id=0, has_side_effects=True, vmem_limit_bytes=60 * 1024 * 1024
        ),
    )(embeddings, owner)


def local(embeddings, owner):
    rows = embeddings.shape[0]
    lines = owner.reshape(rows // 128, 128)
    out, flag = few_slots(embeddings, lines)
    out = lax.cond(flag[0, 0] > FULL / 2, lambda e, o, kept: all_slots(e, o), lambda e, o, kept: kept, embeddings, lines, out)
    return tuple(out[which].reshape(rows) for which in range(3))


def solution(mesh):
    placed = (P(("group", "dev"), None), P(("group", "dev")))
    return jax.shard_map(
        local,
        mesh=mesh,
        in_specs=placed,
        out_specs=(P(("group", "dev")), P(("group", "dev")), P(("group", "dev"))),
        check_vma=False,
    )
```

```python
import functools

import jax
import jax.numpy as jnp
from jax import lax
from jax.experimental import pallas as pl
from jax.experimental.pallas import tpu as pltpu
from jax.sharding import PartitionSpec as P

CAP = 32
DEAD = 2.0
STAGE = 8
PIECE = 1
PACK = 4
BASE = 16
POOL = 64
FULL = 1000.0
ORDER = (0, 3, 1, 2)
LEAD = 8
MESH = pl.DeviceIdType.MESH


def room(step):
    return 64 if step <= 3 else 48 if step <= 6 else 32


def ring_offset(k, nz):
    j = k // 2
    size = (j + 1) // 2
    return jnp.where(j % 2 == 1, size, -size)


def padded(
    emb_hbm,
    owner_hbm,
    out_ref,
    emb,
    owner_ref,
    unit,
    outgoing,
    own,
    before,
    after,
    acc,
    ret,
    got,
    load_sem,
    send_sem,
    recv_sem,
    pair_send,
    pair_recv,
    ret_send,
    ret_recv,
    *,
    groups,
    owners,
):
    rows, width = emb.shape
    nz = owners // 2
    group = lax.axis_index("group")
    me = lax.axis_index("dev")
    mez, mec = me // 2, me % 2
    stages = owners // STAGE
    here = 0

    load_owner = pltpu.make_async_copy(owner_hbm, owner_ref, load_sem.at[0])
    load_owner.start()
    load = pltpu.make_async_copy(emb_hbm, emb, load_sem.at[1])
    load.start()

    def target(k):
        z = (mez + ring_offset(k, nz) + nz) % nz
        return 2 * z + (mec + k) % 2

    def source(k):
        z = (mez - ring_offset(k, nz) + nz) % nz
        return 2 * z + (mec + k) % 2

    barrier = pltpu.get_barrier_semaphore()

    def greet(d, carry):
        pl.semaphore_signal(barrier, inc=1, device_id={"dev": (me + d) % owners}, device_id_type=MESH)
        return carry

    lax.fori_loop(1, owners, greet, 0)
    later = (group + 1) % groups
    earlier = (group + groups - 1) % groups
    pl.semaphore_signal(barrier, inc=1, device_id={"group": later}, device_id_type=MESH)
    pl.semaphore_signal(barrier, inc=1, device_id={"group": earlier}, device_id_type=MESH)

    load_owner.wait()

    owner = jnp.concatenate([owner_ref[a : a + 1, :] for a in range(rows // 128)], axis=1)
    chunk = lax.broadcasted_iota(jnp.int32, (owners, 1), 0)
    cluster = 2 * ((mez + ring_offset(chunk, nz) + nz) % nz) + (mec + chunk) % 2
    hot = owner == cluster
    hot_f = jnp.where(hot, 1.0, 0.0)
    hot_b = hot_f.astype(jnp.bfloat16)
    earlier_row = lax.broadcasted_iota(jnp.int32, (rows, rows), 0) < lax.broadcasted_iota(
        jnp.int32, (rows, rows), 1
    )
    ahead = jnp.dot(
        hot_b, jnp.where(earlier_row, 1.0, 0.0).astype(jnp.bfloat16), preferred_element_type=jnp.float32
    )
    rank = jnp.sum(ahead * hot_f, axis=0, keepdims=True).astype(jnp.int32)
    chunk_of = jnp.sum(hot_f * chunk.astype(jnp.float32), axis=0, keepdims=True).astype(jnp.int32)
    slot_of = chunk_of * CAP + rank
    count = jnp.sum(hot_f, axis=1, keepdims=True)

    load.wait()
    raw = emb[...]
    norm = jnp.sum(raw * raw, axis=-1, keepdims=True)
    unit[...] = (raw * lax.rsqrt(norm + 1e-06)).astype(jnp.bfloat16)

    def dispatch(k):
        return pltpu.make_async_remote_copy(
            src_ref=outgoing.at[k],
            dst_ref=own.at[k],
            send_sem=send_sem.at[k],
            recv_sem=recv_sem.at[k],
            device_id={"dev": target(k)},
            device_id_type=MESH,
        )

    def start_dispatch(k, carry):
        dispatch(k).start()
        return carry

    slot = lax.broadcasted_iota(jnp.int32, (PACK * CAP, 1), 0)
    first = lax.broadcasted_iota(jnp.int32, (CAP, width), 1) == 0
    in_chunk = lax.broadcasted_iota(jnp.int32, (CAP, width), 0).astype(jnp.float32)
    for t in range(owners // PACK):
        pick = jnp.where(slot_of == slot + t * PACK * CAP, 1.0, 0.0).astype(jnp.bfloat16)
        packed = jnp.dot(pick, unit[...], preferred_element_type=jnp.float32)
        for c in range(PACK):
            k = t * PACK + c
            empty = first & (in_chunk >= count[k : k + 1, :])
            piece = jnp.where(empty, DEAD, packed[c * CAP : (c + 1) * CAP, :]).astype(jnp.bfloat16)
            if k == here:
                own[k] = piece
            else:
                outgoing[k] = piece
        if t == 0:
            pl.semaphore_wait(barrier, owners + 1)
        lax.fori_loop(max(t * PACK, 1), (t + 1) * PACK, start_dispatch, 0)

    acc[...] = jnp.full_like(acc, -4.0)

    def forward(p, way):
        part = pl.ds(p * PIECE, PIECE)
        return pltpu.make_async_remote_copy(
            src_ref=own.at[part],
            dst_ref=(before if way == 0 else after).at[part],
            send_sem=pair_send.at[way, p],
            recv_sem=pair_recv.at[way, p],
            device_id={"group": later if way == 0 else earlier},
            device_id_type=MESH,
        )

    def block(which, found, jb, ib, diagonal=False):
        right = found[pl.ds(jb * STAGE, STAGE)].reshape(STAGE * CAP, width)
        left = own[pl.ds(ib * STAGE, STAGE)].reshape(STAGE * CAP, width)
        scores = lax.dot_general(right, left, (((1,), (1,)), ((), ())), preferred_element_type=jnp.float32)
        drop = right[:, :128].astype(jnp.float32)[:, 0:1] > 1.5
        if diagonal:
            size = STAGE * CAP
            drop = drop | (
                lax.broadcasted_iota(jnp.int32, (size, size), 0) == lax.broadcasted_iota(jnp.int32, (size, size), 1)
            )
        scores = jnp.where(drop, -1.0, scores)
        best = jnp.max(scores.reshape(STAGE * CAP // 8, 8, STAGE * CAP), axis=0)
        acc[which, ib] = jnp.maximum(acc[which, ib], best)

    def arrive(t):
        def chunk_arrives(k, carry):
            dispatch(k).wait_recv()
            return carry

        def piece_arrives(p, carry):
            lax.fori_loop(p * PIECE, (p + 1) * PIECE, chunk_arrives, 0)
            forward(p, 0).start()
            forward(p, 1).start()
            return carry

        per = STAGE // PIECE
        if t == 0:
            lax.fori_loop(1, PIECE, chunk_arrives, 0)
            forward(0, 0).start()
            forward(0, 1).start()
            lax.fori_loop(1, per, piece_arrives, 0)
        else:
            lax.fori_loop(t * per, (t + 1) * per, piece_arrives, 0)

    def pair_arrives(t):
        def piece(p, carry):
            forward(p, 0).wait_recv()
            forward(p, 1).wait_recv()
            return carry

        per = STAGE // PIECE
        lax.fori_loop(t * per, (t + 1) * per, piece, 0)

    def both(jb, ib):
        block(1, after, jb, ib)
        block(2, before, jb, ib)

    for t in range(stages):
        arrive(t)
        block(0, own, t, t, diagonal=True)

        def own_blocks(b, carry, t=t):
            block(0, own, t, b)
            block(0, own, b, t)
            return carry

        lax.fori_loop(0, t, own_blocks, 0)
        if t > 0:
            pair_arrives(t - 1)

            def new_rows(b, carry, t=t):
                both(b, t)
                return carry

            def new_found(b, carry, t=t):
                both(t - 1, b)
                return carry

            lax.fori_loop(0, t, new_rows, 0)
            lax.fori_loop(0, t, new_found, 0)
    pair_arrives(stages - 1)

    def last_found(b, carry):
        both(stages - 1, b)
        return carry

    lax.fori_loop(0, stages, last_found, 0)

    tiles = []
    for which in range(3):
        parts = []
        for b in range(stages):
            best = jnp.max(acc[which, b], axis=0, keepdims=True)
            parts += [best[:, h * 128 : (h + 1) * 128] for h in range(STAGE * CAP // 128)]
        tiles.append(jnp.concatenate(parts, axis=0))
    lane = lax.broadcasted_iota(jnp.int32, tiles[0].shape, 1)
    per_tile = 128 // CAP
    for j in range(per_tile):
        moved = [pltpu.roll(tiles[w], (CAP * (w - j)) % 128, 1) if (w - j) % 4 else tiles[w] for w in range(3)]
        mixed = jnp.where(lane < CAP, moved[0], jnp.where(lane < 2 * CAP, moved[1], moved[2]))
        for t in range(owners // per_tile):
            k = per_tile * t + j
            if k == here:
                got[k] = mixed[t : t + 1, :]
            else:
                ret[k] = mixed[t : t + 1, :]

    def give_back(k):
        return pltpu.make_async_remote_copy(
            src_ref=ret.at[k],
            dst_ref=got.at[k],
            send_sem=ret_send.at[k],
            recv_sem=ret_recv.at[k],
            device_id={"dev": source(k)},
            device_id_type=MESH,
        )

    def start_back(k, carry):
        give_back(k).start()
        return carry

    lax.fori_loop(1, owners, start_back, 0)

    def drain(k, carry):
        dispatch(k).wait_send()
        return carry

    lax.fori_loop(1, owners, drain, 0)

    def drain_pair(p, carry):
        forward(p, 0).wait_send()
        forward(p, 1).wait_send()
        return carry

    lax.fori_loop(0, owners // PIECE, drain_pair, 0)

    def wait_back(k, carry):
        give_back(k).wait()
        return carry

    lax.fori_loop(1, owners, wait_back, 0)

    table = got[...].reshape(owners, 128)
    high = table.astype(jnp.bfloat16)
    rest = table - high.astype(jnp.float32)
    middle = rest.astype(jnp.bfloat16)
    low = (rest - middle.astype(jnp.float32)).astype(jnp.bfloat16)
    stacked = jnp.concatenate([high, middle, low], axis=0)
    picks = jnp.concatenate([hot_b, hot_b, hot_b], axis=0)
    found = lax.dot_general(stacked, picks, (((0,), (0,)), ((), ())), preferred_element_type=jnp.float32)
    mine = lax.broadcasted_iota(jnp.int32, (CAP, 1), 0) == rank
    for which in range(3):
        kept = jnp.where(mine, found[which * CAP : (which + 1) * CAP, :], 0.0)
        line = jnp.sum(kept, axis=0, keepdims=True)
        for a in range(rows // 128):
            out_ref[which, a : a + 1, :] = line[:, a * 128 : (a + 1) * 128]


def pooled(
    emb_hbm,
    owner_hbm,
    out_ref,
    flag_ref,
    emb,
    owner_ref,
    unit,
    outgoing,
    side,
    own,
    before,
    after,
    acc,
    ret,
    got,
    pool_out,
    pool,
    key_out,
    keys,
    full,
    load_sem,
    send_sem,
    recv_sem,
    pair_send,
    pair_recv,
    ret_send,
    ret_recv,
    hop_send,
    hop_recv,
    share_send,
    share_recv,
    key_hop_send,
    key_hop_recv,
    key_share_send,
    key_share_recv,
    full_send,
    full_recv,
    side_send,
    side_recv,
    *,
    groups,
    owners,
):
    rows, width = emb.shape
    nz = owners // 2
    group = lax.axis_index("group")
    me = lax.axis_index("dev")
    mez, mec = me // 2, me % 2
    sibling = 2 * mez + 1 - mec
    steps = nz // 2
    per_block = STAGE * CAP // BASE
    blocks = 2 * owners // per_block
    group_of = owners // len(ORDER)

    load_owner = pltpu.make_async_copy(owner_hbm, owner_ref, load_sem.at[0])
    load_owner.start()
    load = pltpu.make_async_copy(emb_hbm, emb, load_sem.at[1])
    load.start()

    def target(k):
        return 2 * ((mez + ring_offset(k, nz) + nz) % nz) + (mec + k) % 2

    def source(k):
        return 2 * ((mez - ring_offset(k, nz) + nz) % nz) + (mec + k) % 2

    barrier = pltpu.get_barrier_semaphore()

    def greet(d, carry):
        pl.semaphore_signal(barrier, inc=1, device_id={"dev": (me + d) % owners}, device_id_type=MESH)
        return carry

    def greet_group(d, carry):
        pl.semaphore_signal(barrier, inc=1, device_id={"group": (group + d) % groups}, device_id_type=MESH)
        return carry

    lax.fori_loop(1, owners, greet, 0)
    lax.fori_loop(1, groups, greet_group, 0)

    load_owner.wait()
    owner = jnp.concatenate([owner_ref[a : a + 1, :] for a in range(rows // 128)], axis=1)
    chunk = lax.broadcasted_iota(jnp.int32, (owners, 1), 0)
    cluster = 2 * ((mez + ring_offset(chunk, nz) + nz) % nz) + (mec + chunk) % 2
    hot_f = jnp.where(owner == cluster, 1.0, 0.0)
    hot_b = hot_f.astype(jnp.bfloat16)
    earlier_row = lax.broadcasted_iota(jnp.int32, (rows, rows), 0) < lax.broadcasted_iota(
        jnp.int32, (rows, rows), 1
    )
    ahead = jnp.dot(
        hot_b, jnp.where(earlier_row, 1.0, 0.0).astype(jnp.bfloat16), preferred_element_type=jnp.float32
    )

    def of_row(per_chunk):
        return jnp.sum(hot_f * per_chunk, axis=0, keepdims=True).astype(jnp.int32)

    rank = of_row(ahead)
    chunk_of = of_row(chunk.astype(jnp.float32))
    count = jnp.sum(hot_f, axis=1, keepdims=True)
    counts = lax.dot_general(
        jnp.ones((8, rows), jnp.bfloat16), hot_b, (((1,), (1,)), ((), ())), preferred_element_type=jnp.float32
    )[0:1, :]

    lane = lax.broadcasted_iota(jnp.int32, (1, owners), 1)
    spill = jnp.where(lane >= 2, jnp.maximum(counts - BASE, 0.0), 0.0)

    def way_of(k):
        return 1 - (k // 2) % 2

    same_way = way_of(lane) == way_of(chunk)
    start = jnp.sum(jnp.where(same_way & (lane > chunk), spill, 0.0), axis=1, keepdims=True)
    filled = jnp.sum(jnp.where(same_way & (lane >= chunk), spill, 0.0), axis=1, keepdims=True)
    step_of = (chunk // 2 + 1) // 2
    space = jnp.full((owners, 1), float(room(1)), jnp.float32)
    for s in range(2, steps + 1):
        space = jnp.where(step_of >= s, float(room(s)), space)
    excess = jnp.max(jnp.where(chunk >= 2, filled - space, -1.0), axis=0, keepdims=True)
    at = of_row(start) + rank - BASE
    spilled = (rank >= BASE) & (chunk_of >= 2) & (at < POOL)
    pool_slot = jnp.where(spilled, way_of(chunk_of) * POOL + at, -1)
    hops = (chunk_of // 2 + 1) // 2
    key = jnp.where(spilled, ((hops - 1) * 2 + chunk_of % 2) * BASE + rank - BASE + 1, 0)
    base_slot = jnp.where(rank < BASE, chunk_of * BASE + rank, -1)
    side_slot = jnp.where((rank >= BASE) & (chunk_of < 2), chunk_of * BASE + rank - BASE, -1)

    def pick(slot_of, count_, start_=0):
        slot = lax.broadcasted_iota(jnp.int32, (count_, 1), 0) + start_
        return jnp.where(slot_of == slot, 1.0, 0.0).astype(jnp.bfloat16)

    pooled_rows = pick(pool_slot, 2 * POOL)
    key_row = lax.dot_general(
        jnp.broadcast_to(key.astype(jnp.float32), (8, rows)).astype(jnp.bfloat16),
        pooled_rows,
        (((1,), (1,)), ((), ())),
        preferred_element_type=jnp.float32,
    )[0:1, :]
    key_out[...] = jnp.where(excess > 0.0, FULL, key_row)

    load.wait()
    raw = emb[...]
    norm = jnp.sum(raw * raw, axis=-1, keepdims=True)
    unit[...] = (raw * lax.rsqrt(norm + 1e-06)).astype(jnp.bfloat16)

    def packed(chosen):
        return jnp.dot(chosen, unit[...], preferred_element_type=jnp.float32)

    pool_out[...] = packed(pooled_rows).astype(jnp.bfloat16).reshape(2, POOL, width)

    def remote(src, dst, send, recv, where):
        return pltpu.make_async_remote_copy(
            src_ref=src, dst_ref=dst, send_sem=send, recv_sem=recv, device_id=where, device_id_type=MESH
        )

    def beyond(way):
        return {"dev": 2 * ((mez + (1, nz - 1)[way]) % nz) + mec}

    def hop(s, way, half_):
        cut = 32 if room(s + 1) > 32 else 16
        part = pl.ds(0, cut) if half_ == 0 else pl.ds(cut, room(s + 1) - cut)
        return remote(
            pool_out.at[way, part] if s == 0 else pool.at[s, way, 0, part],
            pool.at[s + 1, way, 0, part],
            hop_send.at[s, way, half_],
            hop_recv.at[s + 1, way, half_],
            beyond(way),
        )

    def key_hop(s, way):
        return remote(
            key_out if s == 0 else keys.at[s, way, 0],
            keys.at[s + 1, way, 0],
            key_hop_send.at[s, way],
            key_hop_recv.at[s + 1, way],
            beyond(way),
        )

    def share(s, way):
        part = pl.ds(0, room(s))
        return remote(
            pool.at[s, way, 0, part],
            pool.at[s, way, 1, part],
            share_send.at[s, way],
            share_recv.at[s, way],
            {"dev": sibling},
        )

    def key_share(s, way):
        return remote(
            key_out if s == 0 else keys.at[s, way, 0],
            keys.at[s, way, 1],
            key_share_send.at[s, way],
            key_share_recv.at[s, way],
            {"dev": sibling},
        )

    def ways(s):
        return (0, 1) if s < steps else (0,)

    def dispatch(n):
        turn = n // group_of
        part = jnp.int32(ORDER[-1])
        for other in range(len(ORDER) - 1):
            part = jnp.where(turn == other, ORDER[other], part)
        return remote(
            outgoing.at[n],
            own.at[owners + n],
            send_sem.at[n],
            recv_sem.at[n],
            {"dev": target(part * group_of + n % group_of)},
        )

    def start_dispatch(k, carry):
        dispatch(k).start()
        return carry

    def to_side():
        return remote(side, own.at[1], side_send, side_recv, {"dev": sibling})

    def forward(first_, size, sem, way):
        part = pl.ds(first_, size)
        return remote(
            own.at[part],
            (before if way == 0 else after).at[part],
            pair_send.at[way, sem],
            pair_recv.at[way, sem],
            {"group": (group + (1 if way == 0 else groups - 1)) % groups},
        )

    def tail_piece(s):
        if s == 0:
            return (0, 2, 0)
        return (4 * s - 2, 4 if s < steps else 2, s)

    def base_piece(p):
        return (owners + 2 * p, 2, steps + 1 + p)

    pl.semaphore_wait(barrier, owners + groups - 2)
    for way in (0, 1):
        key_hop(0, way).start()
    for half_ in (0, 1):
        for way in (0, 1):
            hop(0, way, half_).start()
    key_share(0, 0).start()

    in_piece = lax.broadcasted_iota(jnp.int32, (BASE, width), 0).astype(jnp.float32)
    first = lax.broadcasted_iota(jnp.int32, (BASE, width), 1) == 0

    def with_mark(values, k, offset):
        empty = first & (in_piece + offset >= count[k : k + 1, :])
        return jnp.where(empty, DEAD, values).astype(jnp.bfloat16)

    for t in range(owners // group_of):
        values = packed(pick(base_slot, group_of * BASE, ORDER[t] * group_of * BASE))
        for c in range(group_of):
            n = t * group_of + c
            piece = with_mark(values[c * BASE : (c + 1) * BASE, :], ORDER[t] * group_of + c, 0.0)
            if n == 0:
                own[owners] = piece
            else:
                outgoing[n] = piece
        if t == 0:
            lax.fori_loop(1, LEAD, start_dispatch, 0)
    values = packed(pick(side_slot, 2 * BASE))
    own[0] = with_mark(values[:BASE, :], 0, float(BASE))
    side[...] = with_mark(values[BASE:, :], 1, float(BASE))
    to_side().start()
    acc[...] = jnp.full_like(acc, -4.0)
    for s in range(1, steps + 1):
        if room(s) < POOL:
            for way in ways(s):
                for core in (0, 1):
                    pool[s, way, core, room(s) :] = jnp.zeros((POOL - room(s), width), jnp.bfloat16)

    def forward_both(piece):
        forward(*piece, 0).start()
        forward(*piece, 1).start()

    def base_arrives(p, carry):
        def one(k, inner):
            dispatch(k).wait_recv()
            return inner

        lax.fori_loop(2 * p, 2 * p + 2, one, 0)
        forward_both(base_piece(p))
        return carry

    def block(which, found, jb, ib, diagonal=False):
        right = found[pl.ds(jb * per_block, per_block)].reshape(per_block * BASE, width)
        left = own[pl.ds(ib * per_block, per_block)].reshape(per_block * BASE, width)
        scores = lax.dot_general(right, left, (((1,), (1,)), ((), ())), preferred_element_type=jnp.float32)
        drop = right[:, :128].astype(jnp.float32)[:, 0:1] > 1.5
        size = per_block * BASE
        if diagonal:
            drop = drop | (
                (jb == ib)
                & (
                    lax.broadcasted_iota(jnp.int32, (size, size), 0)
                    == lax.broadcasted_iota(jnp.int32, (size, size), 1)
                )
            )
        scores = jnp.where(drop, -1.0, scores)
        best = jnp.max(scores.reshape(size // 8, 8, size), axis=0)
        acc[which, ib] = jnp.maximum(acc[which, ib], best)

    def run(combos, kind, stride_j, start_j, stride_i, start_i):
        across = 2 if stride_i == 2 else blocks

        def body(x, carry):
            jb = stride_j * (x // across) + start_j
            ib = stride_i * (x % across) + start_i
            if kind == "own":
                block(0, own, jb, ib, diagonal=True)
            else:
                block(1, after, jb, ib)
                block(2, before, jb, ib)
            return carry

        lax.fori_loop(0, combos, body, 0)

    wide = lax.broadcasted_iota(jnp.int32, (1, 4 * POOL), 1)
    tall = lax.broadcasted_iota(jnp.int32, (4 * BASE, 1), 0)
    narrow = lax.broadcasted_iota(jnp.int32, (1, 128), 1)

    def select(s):
        parts = []
        for way in ways(s):
            zero, one = keys[s, way, 0], keys[s, way, 1]
            if way == 0:
                parts.append(jnp.where(narrow < POOL, zero, pltpu.roll(one, POOL, 1)))
            else:
                parts.append(jnp.where(narrow < POOL, pltpu.roll(zero, POOL, 1), one))
        n = len(parts)
        held = jnp.concatenate(parts, axis=1)
        lanes, outs = wide[:, : 2 * n * POOL], tall[: 2 * n * BASE, :]
        wanted = (((s - 1) * 2 + (outs // BASE) % 2) * BASE + outs % BASE + 1).astype(jnp.float32)
        match = (lanes // POOL == outs // BASE) & (held == wanted)
        chosen = jnp.where(match, 1.0, 0.0)
        there = pool[s, 0:n].reshape(2 * n * POOL, width)
        values_ = jnp.dot(chosen.astype(jnp.bfloat16), there, preferred_element_type=jnp.float32)
        none = jnp.sum(chosen, axis=1, keepdims=True) < 0.5
        front = lax.broadcasted_iota(jnp.int32, values_.shape, 1) == 0
        values_ = jnp.where(front & none, DEAD, values_).astype(jnp.bfloat16)
        begin, size, _ = tail_piece(s)
        own[begin : begin + size] = values_.reshape(size, BASE, width)

    to_side().wait_recv()
    forward_both(tail_piece(0))
    for s in range(1, steps + 1):
        for half_ in (0, 1):
            for way in ways(s):
                hop(s - 1, way, half_).wait_recv()
                if s < steps - way:
                    hop(s, way, half_).start()
        for way in ways(s):
            key_hop(s - 1, way).wait_recv()
            if s < steps - way:
                key_hop(s, way).start()
            key_share(s, way).start()
            share(s, way).start()
        if s < steps:
            per_step = (owners - LEAD + steps - 2) // (steps - 1)
            low = min(LEAD + per_step * (s - 1), owners)
            lax.fori_loop(low, min(low + per_step, owners), start_dispatch, 0)
        for way in ways(s):
            share(s, way).wait_recv()
            key_share(s, way).wait_recv()
        select(s)
        forward_both(tail_piece(s))
        if s == 2:
            dispatch(1).wait_recv()
            forward_both(base_piece(0))
        if s > 2:
            lax.fori_loop(2 * s - 5, 2 * s - 3, base_arrives, 0)
        if s == steps - 2:
            run(4, "own", 2, 0, 2, 0)
    key_share(0, 0).wait_recv()

    worst = jnp.maximum(key_out[...], keys[0, 0, 1])
    for s in range(1, steps + 1):
        for way in ways(s):
            worst = jnp.maximum(worst, jnp.maximum(keys[s, way, 0], keys[s, way, 1]))
    full[0] = worst

    def tell(d):
        return remote(
            full.at[0], full.at[d], full_send.at[d], full_recv.at[d], {"group": (group + d) % groups}
        )

    def start_tell(d, carry):
        tell(d).start()
        return carry

    lax.fori_loop(1, groups, start_tell, 0)

    def pair_arrives(pieces):
        for piece in pieces:
            forward(*piece, 0).wait_recv()
            forward(*piece, 1).wait_recv()

    def base_pair_arrives(p, carry):
        pair_arrives([base_piece(p)])
        return carry

    half = steps // 2
    done = 2 * steps - 3
    lax.fori_loop(done, done + 1, base_arrives, 0)
    pair_arrives([tail_piece(s) for s in range(half + 1)])
    lax.fori_loop(0, half * 2, base_pair_arrives, 0)
    run(4, "pair", 2, 0, 2, 0)
    lax.fori_loop(done + 1, owners // 2, base_arrives, 0)
    run(8, "own", 2, 1, 1, 0)
    run(4, "own", 2, 0, 2, 1)
    run(4, "pair", 2, 0, 2, 1)
    pair_arrives([tail_piece(s) for s in range(half + 1, steps + 1)])
    run(4, "pair", 0, 1, 1, 0)
    lax.fori_loop(half * 2, owners // 2, base_pair_arrives, 0)
    run(4, "pair", 0, 3, 1, 0)

    tiles = []
    for which in range(3):
        parts = []
        for b in range(blocks):
            best = jnp.max(acc[which, b], axis=0, keepdims=True)
            parts += [best[:, h * 128 : (h + 1) * 128] for h in range(per_block * BASE // 128)]
        early = jnp.concatenate([parts[len(parts) // 2 + ORDER.index(t)] for t in range(len(ORDER))], axis=0)
        late = jnp.concatenate(parts[: len(parts) // 2], axis=0)
        tiles += [early, late]
    spot = lax.broadcasted_iota(jnp.int32, tiles[0].shape, 1) // BASE
    per_tile = 128 // BASE
    for j in range(per_tile):
        mixed = tiles[0] if j == 0 else pltpu.roll(tiles[0], (-BASE * j) % 128, 1)
        for u in range(1, 6):
            moved = tiles[u] if u == j else pltpu.roll(tiles[u], (BASE * (u - j)) % 128, 1)
            mixed = jnp.where(spot >= u, moved, mixed)
        for t in range(owners // per_tile):
            k = per_tile * t + j
            if k == 0:
                got[k] = mixed[t : t + 1, :]
            else:
                ret[k] = mixed[t : t + 1, :]

    def give_back(k):
        return remote(ret.at[k], got.at[k], ret_send.at[k], ret_recv.at[k], {"dev": source(k)})

    def start_back(k, carry):
        give_back(owners - k).start()
        return carry

    lax.fori_loop(1, owners, start_back, 0)

    def drain(k, carry):
        dispatch(k).wait_send()
        return carry

    lax.fori_loop(1, owners, drain, 0)
    to_side().wait_send()
    key_share(0, 0).wait_send()
    for s in range(steps + 1):
        for way in (0, 1):
            if s < steps - way:
                hop(s, way, 0).wait_send()
                hop(s, way, 1).wait_send()
                key_hop(s, way).wait_send()
        if s > 0:
            for way in ways(s):
                share(s, way).wait_send()
                key_share(s, way).wait_send()
        forward(*tail_piece(s), 0).wait_send()
        forward(*tail_piece(s), 1).wait_send()

    def drain_pair(p, carry):
        forward(*base_piece(p), 0).wait_send()
        forward(*base_piece(p), 1).wait_send()
        return carry

    lax.fori_loop(0, owners // 2, drain_pair, 0)

    def wait_tell(d, carry):
        tell(d).wait()
        return carry

    lax.fori_loop(1, groups, wait_tell, 0)
    flag_ref[0, 0] = jnp.max(full[...])

    def wait_back(k, carry):
        give_back(k).wait()
        return carry

    lax.fori_loop(1, owners, wait_back, 0)

    table = got[...].reshape(owners, 128)
    high = table.astype(jnp.bfloat16)
    rest = table - high.astype(jnp.float32)
    middle = rest.astype(jnp.bfloat16)
    low_part = (rest - middle.astype(jnp.float32)).astype(jnp.bfloat16)
    stacked = jnp.concatenate([high, middle, low_part], axis=0)
    picks = jnp.concatenate([hot_b, hot_b, hot_b], axis=0)
    found = lax.dot_general(stacked, picks, (((0,), (0,)), ((), ())), preferred_element_type=jnp.float32)
    mine = lax.broadcasted_iota(jnp.int32, (CAP, 1), 0) == rank
    for which in range(3):
        kept = jnp.where(mine, found[which * CAP : (which + 1) * CAP, :], 0.0)
        line = jnp.sum(kept, axis=0, keepdims=True)
        for a in range(rows // 128):
            out_ref[which, a : a + 1, :] = line[:, a * 128 : (a + 1) * 128]


def all_slots(embeddings, owner):
    owners = lax.axis_size("dev")
    groups = lax.axis_size("group")
    rows, width = embeddings.shape
    vmem = pl.BlockSpec(memory_space=pltpu.VMEM)
    slots = (owners, CAP, width)
    hbm = pl.BlockSpec(memory_space=pltpu.HBM)
    return pl.pallas_call(
        functools.partial(padded, groups=groups, owners=owners),
        out_shape=jax.ShapeDtypeStruct((3, rows // 128, 128), jnp.float32),
        in_specs=[hbm, hbm],
        out_specs=vmem,
        scratch_shapes=[
            pltpu.VMEM((rows, width), jnp.float32),
            pltpu.VMEM((rows // 128, 128), jnp.int32),
            pltpu.VMEM((rows, width), jnp.bfloat16),
            pltpu.VMEM(slots, jnp.bfloat16),
            pltpu.VMEM(slots, jnp.bfloat16),
            pltpu.VMEM(slots, jnp.bfloat16),
            pltpu.VMEM(slots, jnp.bfloat16),
            pltpu.VMEM((3, owners // STAGE, 8, STAGE * CAP), jnp.float32),
            pltpu.VMEM((owners, 1, 128), jnp.float32),
            pltpu.VMEM((owners, 1, 128), jnp.float32),
            pltpu.SemaphoreType.DMA((2,)),
            pltpu.SemaphoreType.DMA((owners,)),
            pltpu.SemaphoreType.DMA((owners,)),
            pltpu.SemaphoreType.DMA((2, owners // PIECE)),
            pltpu.SemaphoreType.DMA((2, owners // PIECE)),
            pltpu.SemaphoreType.DMA((owners,)),
            pltpu.SemaphoreType.DMA((owners,)),
        ],
        compiler_params=pltpu.CompilerParams(
            collective_id=1, has_side_effects=True, vmem_limit_bytes=60 * 1024 * 1024
        ),
    )(embeddings, owner)


def few_slots(embeddings, owner):
    owners = lax.axis_size("dev")
    groups = lax.axis_size("group")
    rows, width = embeddings.shape
    steps = owners // 4
    vmem = pl.BlockSpec(memory_space=pltpu.VMEM)
    hbm = pl.BlockSpec(memory_space=pltpu.HBM)
    entries = (2 * owners, BASE, width)
    size = STAGE * CAP
    pieces = steps + 1 + owners // 2
    ring = pltpu.SemaphoreType.DMA((steps + 1, 2))
    halves = pltpu.SemaphoreType.DMA((steps + 1, 2, 2))
    return pl.pallas_call(
        functools.partial(pooled, groups=groups, owners=owners),
        out_shape=(
            jax.ShapeDtypeStruct((3, rows // 128, 128), jnp.float32),
            jax.ShapeDtypeStruct((1, 1), jnp.float32),
        ),
        in_specs=[hbm, hbm],
        out_specs=(vmem, pl.BlockSpec(memory_space=pltpu.SMEM)),
        scratch_shapes=[
            pltpu.VMEM((rows, width), jnp.float32),
            pltpu.VMEM((rows // 128, 128), jnp.int32),
            pltpu.VMEM((rows, width), jnp.bfloat16),
            pltpu.VMEM((owners, BASE, width), jnp.bfloat16),
            pltpu.VMEM((BASE, width), jnp.bfloat16),
            pltpu.VMEM(entries, jnp.bfloat16),
            pltpu.VMEM(entries, jnp.bfloat16),
            pltpu.VMEM(entries, jnp.bfloat16),
            pltpu.VMEM((3, 2 * owners * BASE // size, 8, size), jnp.float32),
            pltpu.VMEM((owners, 1, 128), jnp.float32),
            pltpu.VMEM((owners, 1, 128), jnp.float32),
            pltpu.VMEM((2, POOL, width), jnp.bfloat16),
            pltpu.VMEM((steps + 1, 2, 2, POOL, width), jnp.bfloat16),
            pltpu.VMEM((1, 128), jnp.float32),
            pltpu.VMEM((steps + 1, 2, 2, 1, 128), jnp.float32),
            pltpu.VMEM((groups, 1, 128), jnp.float32),
            pltpu.SemaphoreType.DMA((2,)),
            pltpu.SemaphoreType.DMA((owners,)),
            pltpu.SemaphoreType.DMA((owners,)),
            pltpu.SemaphoreType.DMA((2, pieces)),
            pltpu.SemaphoreType.DMA((2, pieces)),
            pltpu.SemaphoreType.DMA((owners,)),
            pltpu.SemaphoreType.DMA((owners,)),
            halves,
            halves,
            ring,
            ring,
            ring,
            ring,
            ring,
            ring,
            pltpu.SemaphoreType.DMA((groups,)),
            pltpu.SemaphoreType.DMA((groups,)),
            pltpu.SemaphoreType.DMA,
            pltpu.SemaphoreType.DMA,
        ],
        compiler_params=pltpu.CompilerParams(
            collective_id=0, has_side_effects=True, vmem_limit_bytes=60 * 1024 * 1024
        ),
    )(embeddings, owner)


def local(embeddings, owner):
    rows = embeddings.shape[0]
    lines = owner.reshape(rows // 128, 128)
    out, flag = few_slots(embeddings, lines)
    out = lax.cond(flag[0, 0] > FULL / 2, lambda e, o, kept: all_slots(e, o), lambda e, o, kept: kept, embeddings, lines, out)
    return tuple(out[which].reshape(rows) for which in range(3))


def solution(mesh):
    placed = (P(("group", "dev"), None), P(("group", "dev")))
    return jax.shard_map(
        local,
        mesh=mesh,
        in_specs=placed,
        out_specs=(P(("group", "dev")), P(("group", "dev")), P(("group", "dev"))),
        check_vma=False,
    )
```

```python
import functools

import jax
import jax.numpy as jnp
from jax import lax
from jax.experimental import pallas as pl
from jax.experimental.pallas import tpu as pltpu
from jax.sharding import PartitionSpec as P

CAP = 32
DEAD = 2.0
STAGE = 8
PIECE = 1
PACK = 4
BASE = 16
POOL = 64
FULL = 1000.0
ORDER = (0, 3, 1, 2)
LEAD = 8
MESH = pl.DeviceIdType.MESH


def room(step):
    return 64 if step <= 3 else 48 if step <= 6 else 32


def ring_offset(k, nz):
    j = k // 2
    size = (j + 1) // 2
    return jnp.where(j % 2 == 1, size, -size)


def padded(
    emb_hbm,
    owner_hbm,
    out_ref,
    emb,
    owner_ref,
    unit,
    outgoing,
    own,
    before,
    after,
    acc,
    ret,
    got,
    load_sem,
    send_sem,
    recv_sem,
    pair_send,
    pair_recv,
    ret_send,
    ret_recv,
    *,
    groups,
    owners,
):
    rows, width = emb.shape
    nz = owners // 2
    group = lax.axis_index("group")
    me = lax.axis_index("dev")
    mez, mec = me // 2, me % 2
    stages = owners // STAGE
    here = 0

    load_owner = pltpu.make_async_copy(owner_hbm, owner_ref, load_sem.at[0])
    load_owner.start()
    load = pltpu.make_async_copy(emb_hbm, emb, load_sem.at[1])
    load.start()

    def target(k):
        z = (mez + ring_offset(k, nz) + nz) % nz
        return 2 * z + (mec + k) % 2

    def source(k):
        z = (mez - ring_offset(k, nz) + nz) % nz
        return 2 * z + (mec + k) % 2

    barrier = pltpu.get_barrier_semaphore()

    def greet(d, carry):
        pl.semaphore_signal(barrier, inc=1, device_id={"dev": (me + d) % owners}, device_id_type=MESH)
        return carry

    lax.fori_loop(1, owners, greet, 0)
    later = (group + 1) % groups
    earlier = (group + groups - 1) % groups
    pl.semaphore_signal(barrier, inc=1, device_id={"group": later}, device_id_type=MESH)
    pl.semaphore_signal(barrier, inc=1, device_id={"group": earlier}, device_id_type=MESH)

    load_owner.wait()

    owner = jnp.concatenate([owner_ref[a : a + 1, :] for a in range(rows // 128)], axis=1)
    chunk = lax.broadcasted_iota(jnp.int32, (owners, 1), 0)
    cluster = 2 * ((mez + ring_offset(chunk, nz) + nz) % nz) + (mec + chunk) % 2
    hot = owner == cluster
    hot_f = jnp.where(hot, 1.0, 0.0)
    hot_b = hot_f.astype(jnp.bfloat16)
    earlier_row = lax.broadcasted_iota(jnp.int32, (rows, rows), 0) < lax.broadcasted_iota(
        jnp.int32, (rows, rows), 1
    )
    ahead = jnp.dot(
        hot_b, jnp.where(earlier_row, 1.0, 0.0).astype(jnp.bfloat16), preferred_element_type=jnp.float32
    )
    rank = jnp.sum(ahead * hot_f, axis=0, keepdims=True).astype(jnp.int32)
    chunk_of = jnp.sum(hot_f * chunk.astype(jnp.float32), axis=0, keepdims=True).astype(jnp.int32)
    slot_of = chunk_of * CAP + rank
    count = jnp.sum(hot_f, axis=1, keepdims=True)

    load.wait()
    raw = emb[...]
    norm = jnp.sum(raw * raw, axis=-1, keepdims=True)
    unit[...] = (raw * lax.rsqrt(norm + 1e-06)).astype(jnp.bfloat16)

    def dispatch(k):
        return pltpu.make_async_remote_copy(
            src_ref=outgoing.at[k],
            dst_ref=own.at[k],
            send_sem=send_sem.at[k],
            recv_sem=recv_sem.at[k],
            device_id={"dev": target(k)},
            device_id_type=MESH,
        )

    def start_dispatch(k, carry):
        dispatch(k).start()
        return carry

    slot = lax.broadcasted_iota(jnp.int32, (PACK * CAP, 1), 0)
    first = lax.broadcasted_iota(jnp.int32, (CAP, width), 1) == 0
    in_chunk = lax.broadcasted_iota(jnp.int32, (CAP, width), 0).astype(jnp.float32)
    for t in range(owners // PACK):
        pick = jnp.where(slot_of == slot + t * PACK * CAP, 1.0, 0.0).astype(jnp.bfloat16)
        packed = jnp.dot(pick, unit[...], preferred_element_type=jnp.float32)
        for c in range(PACK):
            k = t * PACK + c
            empty = first & (in_chunk >= count[k : k + 1, :])
            piece = jnp.where(empty, DEAD, packed[c * CAP : (c + 1) * CAP, :]).astype(jnp.bfloat16)
            if k == here:
                own[k] = piece
            else:
                outgoing[k] = piece
        if t == 0:
            pl.semaphore_wait(barrier, owners + 1)
        lax.fori_loop(max(t * PACK, 1), (t + 1) * PACK, start_dispatch, 0)

    acc[...] = jnp.full_like(acc, -4.0)

    def forward(p, way):
        part = pl.ds(p * PIECE, PIECE)
        return pltpu.make_async_remote_copy(
            src_ref=own.at[part],
            dst_ref=(before if way == 0 else after).at[part],
            send_sem=pair_send.at[way, p],
            recv_sem=pair_recv.at[way, p],
            device_id={"group": later if way == 0 else earlier},
            device_id_type=MESH,
        )

    def block(which, found, jb, ib, diagonal=False):
        right = found[pl.ds(jb * STAGE, STAGE)].reshape(STAGE * CAP, width)
        left = own[pl.ds(ib * STAGE, STAGE)].reshape(STAGE * CAP, width)
        scores = lax.dot_general(right, left, (((1,), (1,)), ((), ())), preferred_element_type=jnp.float32)
        drop = right[:, :128].astype(jnp.float32)[:, 0:1] > 1.5
        if diagonal:
            size = STAGE * CAP
            drop = drop | (
                lax.broadcasted_iota(jnp.int32, (size, size), 0) == lax.broadcasted_iota(jnp.int32, (size, size), 1)
            )
        scores = jnp.where(drop, -1.0, scores)
        best = jnp.max(scores.reshape(STAGE * CAP // 8, 8, STAGE * CAP), axis=0)
        acc[which, ib] = jnp.maximum(acc[which, ib], best)

    def arrive(t):
        def chunk_arrives(k, carry):
            dispatch(k).wait_recv()
            return carry

        def piece_arrives(p, carry):
            lax.fori_loop(p * PIECE, (p + 1) * PIECE, chunk_arrives, 0)
            forward(p, 0).start()
            forward(p, 1).start()
            return carry

        per = STAGE // PIECE
        if t == 0:
            lax.fori_loop(1, PIECE, chunk_arrives, 0)
            forward(0, 0).start()
            forward(0, 1).start()
            lax.fori_loop(1, per, piece_arrives, 0)
        else:
            lax.fori_loop(t * per, (t + 1) * per, piece_arrives, 0)

    def pair_arrives(t):
        def piece(p, carry):
            forward(p, 0).wait_recv()
            forward(p, 1).wait_recv()
            return carry

        per = STAGE // PIECE
        lax.fori_loop(t * per, (t + 1) * per, piece, 0)

    def both(jb, ib):
        block(1, after, jb, ib)
        block(2, before, jb, ib)

    for t in range(stages):
        arrive(t)
        block(0, own, t, t, diagonal=True)

        def own_blocks(b, carry, t=t):
            block(0, own, t, b)
            block(0, own, b, t)
            return carry

        lax.fori_loop(0, t, own_blocks, 0)
        if t > 0:
            pair_arrives(t - 1)

            def new_rows(b, carry, t=t):
                both(b, t)
                return carry

            def new_found(b, carry, t=t):
                both(t - 1, b)
                return carry

            lax.fori_loop(0, t, new_rows, 0)
            lax.fori_loop(0, t, new_found, 0)
    pair_arrives(stages - 1)

    def last_found(b, carry):
        both(stages - 1, b)
        return carry

    lax.fori_loop(0, stages, last_found, 0)

    tiles = []
    for which in range(3):
        parts = []
        for b in range(stages):
            best = jnp.max(acc[which, b], axis=0, keepdims=True)
            parts += [best[:, h * 128 : (h + 1) * 128] for h in range(STAGE * CAP // 128)]
        tiles.append(jnp.concatenate(parts, axis=0))
    lane = lax.broadcasted_iota(jnp.int32, tiles[0].shape, 1)
    per_tile = 128 // CAP
    for j in range(per_tile):
        moved = [pltpu.roll(tiles[w], (CAP * (w - j)) % 128, 1) if (w - j) % 4 else tiles[w] for w in range(3)]
        mixed = jnp.where(lane < CAP, moved[0], jnp.where(lane < 2 * CAP, moved[1], moved[2]))
        for t in range(owners // per_tile):
            k = per_tile * t + j
            if k == here:
                got[k] = mixed[t : t + 1, :]
            else:
                ret[k] = mixed[t : t + 1, :]

    def give_back(k):
        return pltpu.make_async_remote_copy(
            src_ref=ret.at[k],
            dst_ref=got.at[k],
            send_sem=ret_send.at[k],
            recv_sem=ret_recv.at[k],
            device_id={"dev": source(k)},
            device_id_type=MESH,
        )

    def start_back(k, carry):
        give_back(k).start()
        return carry

    lax.fori_loop(1, owners, start_back, 0)

    def drain(k, carry):
        dispatch(k).wait_send()
        return carry

    lax.fori_loop(1, owners, drain, 0)

    def drain_pair(p, carry):
        forward(p, 0).wait_send()
        forward(p, 1).wait_send()
        return carry

    lax.fori_loop(0, owners // PIECE, drain_pair, 0)

    def wait_back(k, carry):
        give_back(k).wait()
        return carry

    lax.fori_loop(1, owners, wait_back, 0)

    table = got[...].reshape(owners, 128)
    high = table.astype(jnp.bfloat16)
    rest = table - high.astype(jnp.float32)
    middle = rest.astype(jnp.bfloat16)
    low = (rest - middle.astype(jnp.float32)).astype(jnp.bfloat16)
    stacked = jnp.concatenate([high, middle, low], axis=0)
    picks = jnp.concatenate([hot_b, hot_b, hot_b], axis=0)
    found = lax.dot_general(stacked, picks, (((0,), (0,)), ((), ())), preferred_element_type=jnp.float32)
    mine = lax.broadcasted_iota(jnp.int32, (CAP, 1), 0) == rank
    for which in range(3):
        kept = jnp.where(mine, found[which * CAP : (which + 1) * CAP, :], 0.0)
        line = jnp.sum(kept, axis=0, keepdims=True)
        for a in range(rows // 128):
            out_ref[which, a : a + 1, :] = line[:, a * 128 : (a + 1) * 128]


def pooled(
    emb_hbm,
    owner_hbm,
    out_ref,
    flag_ref,
    emb,
    owner_ref,
    unit,
    outgoing,
    side,
    own,
    before,
    after,
    acc,
    ret,
    got,
    pool_out,
    pool,
    key_out,
    keys,
    full,
    load_sem,
    send_sem,
    recv_sem,
    pair_send,
    pair_recv,
    ret_send,
    ret_recv,
    hop_send,
    hop_recv,
    share_send,
    share_recv,
    key_hop_send,
    key_hop_recv,
    key_share_send,
    key_share_recv,
    full_send,
    full_recv,
    side_send,
    side_recv,
    *,
    groups,
    owners,
):
    rows, width = emb.shape
    nz = owners // 2
    group = lax.axis_index("group")
    me = lax.axis_index("dev")
    mez, mec = me // 2, me % 2
    sibling = 2 * mez + 1 - mec
    steps = nz // 2
    per_block = STAGE * CAP // BASE
    blocks = 2 * owners // per_block
    group_of = owners // len(ORDER)

    load_owner = pltpu.make_async_copy(owner_hbm, owner_ref, load_sem.at[0])
    load_owner.start()
    load = pltpu.make_async_copy(emb_hbm, emb, load_sem.at[1])
    load.start()

    def target(k):
        return 2 * ((mez + ring_offset(k, nz) + nz) % nz) + (mec + k) % 2

    def source(k):
        return 2 * ((mez - ring_offset(k, nz) + nz) % nz) + (mec + k) % 2

    barrier = pltpu.get_barrier_semaphore()

    def greet(d, carry):
        pl.semaphore_signal(barrier, inc=1, device_id={"dev": (me + d) % owners}, device_id_type=MESH)
        return carry

    def greet_group(d, carry):
        pl.semaphore_signal(barrier, inc=1, device_id={"group": (group + d) % groups}, device_id_type=MESH)
        return carry

    lax.fori_loop(1, owners, greet, 0)
    lax.fori_loop(1, groups, greet_group, 0)

    load_owner.wait()
    owner = jnp.concatenate([owner_ref[a : a + 1, :] for a in range(rows // 128)], axis=1)
    chunk = lax.broadcasted_iota(jnp.int32, (owners, 1), 0)
    cluster = 2 * ((mez + ring_offset(chunk, nz) + nz) % nz) + (mec + chunk) % 2
    hot_f = jnp.where(owner == cluster, 1.0, 0.0)
    hot_b = hot_f.astype(jnp.bfloat16)
    earlier_row = lax.broadcasted_iota(jnp.int32, (rows, rows), 0) < lax.broadcasted_iota(
        jnp.int32, (rows, rows), 1
    )
    ahead = jnp.dot(
        hot_b, jnp.where(earlier_row, 1.0, 0.0).astype(jnp.bfloat16), preferred_element_type=jnp.float32
    )

    def of_row(per_chunk):
        return jnp.sum(hot_f * per_chunk, axis=0, keepdims=True).astype(jnp.int32)

    rank = of_row(ahead)
    chunk_of = of_row(chunk.astype(jnp.float32))
    count = jnp.sum(hot_f, axis=1, keepdims=True)
    counts = lax.dot_general(
        jnp.ones((8, rows), jnp.bfloat16), hot_b, (((1,), (1,)), ((), ())), preferred_element_type=jnp.float32
    )[0:1, :]

    lane = lax.broadcasted_iota(jnp.int32, (1, owners), 1)
    spill = jnp.where(lane >= 2, jnp.maximum(counts - BASE, 0.0), 0.0)

    def way_of(k):
        return 1 - (k // 2) % 2

    same_way = way_of(lane) == way_of(chunk)
    start = jnp.sum(jnp.where(same_way & (lane > chunk), spill, 0.0), axis=1, keepdims=True)
    filled = jnp.sum(jnp.where(same_way & (lane >= chunk), spill, 0.0), axis=1, keepdims=True)
    step_of = (chunk // 2 + 1) // 2
    space = jnp.full((owners, 1), float(room(1)), jnp.float32)
    for s in range(2, steps + 1):
        space = jnp.where(step_of >= s, float(room(s)), space)
    excess = jnp.max(jnp.where(chunk >= 2, filled - space, -1.0), axis=0, keepdims=True)
    at = of_row(start) + rank - BASE
    spilled = (rank >= BASE) & (chunk_of >= 2) & (at < POOL)
    pool_slot = jnp.where(spilled, way_of(chunk_of) * POOL + at, -1)
    hops = (chunk_of // 2 + 1) // 2
    key = jnp.where(spilled, ((hops - 1) * 2 + chunk_of % 2) * BASE + rank - BASE + 1, 0)
    base_slot = jnp.where(rank < BASE, chunk_of * BASE + rank, -1)
    side_slot = jnp.where((rank >= BASE) & (chunk_of < 2), chunk_of * BASE + rank - BASE, -1)

    def pick(slot_of, count_, start_=0):
        slot = lax.broadcasted_iota(jnp.int32, (count_, 1), 0) + start_
        return jnp.where(slot_of == slot, 1.0, 0.0).astype(jnp.bfloat16)

    pooled_rows = pick(pool_slot, 2 * POOL)
    key_row = lax.dot_general(
        jnp.broadcast_to(key.astype(jnp.float32), (8, rows)).astype(jnp.bfloat16),
        pooled_rows,
        (((1,), (1,)), ((), ())),
        preferred_element_type=jnp.float32,
    )[0:1, :]
    key_out[...] = jnp.where(excess > 0.0, FULL, key_row)

    load.wait()
    raw = emb[...]
    norm = jnp.sum(raw * raw, axis=-1, keepdims=True)
    unit[...] = (raw * lax.rsqrt(norm + 1e-06)).astype(jnp.bfloat16)

    def packed(chosen):
        return jnp.dot(chosen, unit[...], preferred_element_type=jnp.float32)

    pool_out[...] = packed(pooled_rows).astype(jnp.bfloat16).reshape(2, POOL, width)

    def remote(src, dst, send, recv, where):
        return pltpu.make_async_remote_copy(
            src_ref=src, dst_ref=dst, send_sem=send, recv_sem=recv, device_id=where, device_id_type=MESH
        )

    def beyond(way):
        return {"dev": 2 * ((mez + (1, nz - 1)[way]) % nz) + mec}

    def hop(s, way, half_):
        cut = 32 if room(s + 1) > 32 else 16
        part = pl.ds(0, cut) if half_ == 0 else pl.ds(cut, room(s + 1) - cut)
        return remote(
            pool_out.at[way, part] if s == 0 else pool.at[s, way, 0, part],
            pool.at[s + 1, way, 0, part],
            hop_send.at[s, way, half_],
            hop_recv.at[s + 1, way, half_],
            beyond(way),
        )

    def key_hop(s, way):
        return remote(
            key_out if s == 0 else keys.at[s, way, 0],
            keys.at[s + 1, way, 0],
            key_hop_send.at[s, way],
            key_hop_recv.at[s + 1, way],
            beyond(way),
        )

    def share(s, way):
        part = pl.ds(0, room(s))
        return remote(
            pool.at[s, way, 0, part],
            pool.at[s, way, 1, part],
            share_send.at[s, way],
            share_recv.at[s, way],
            {"dev": sibling},
        )

    def key_share(s, way):
        return remote(
            key_out if s == 0 else keys.at[s, way, 0],
            keys.at[s, way, 1],
            key_share_send.at[s, way],
            key_share_recv.at[s, way],
            {"dev": sibling},
        )

    def ways(s):
        return (0, 1) if s < steps else (0,)

    def dispatch(n):
        turn = n // group_of
        part = jnp.int32(ORDER[-1])
        for other in range(len(ORDER) - 1):
            part = jnp.where(turn == other, ORDER[other], part)
        return remote(
            outgoing.at[n],
            own.at[owners + n],
            send_sem.at[n],
            recv_sem.at[n],
            {"dev": target(part * group_of + n % group_of)},
        )

    def start_dispatch(k, carry):
        dispatch(k).start()
        return carry

    def to_side():
        return remote(side, own.at[1], side_send, side_recv, {"dev": sibling})

    def forward(first_, size, sem, way):
        part = pl.ds(first_, size)
        return remote(
            own.at[part],
            (before if way == 0 else after).at[part],
            pair_send.at[way, sem],
            pair_recv.at[way, sem],
            {"group": (group + (1 if way == 0 else groups - 1)) % groups},
        )

    def tail_piece(s):
        if s == 0:
            return (0, 2, 0)
        return (4 * s - 2, 4 if s < steps else 2, s)

    def base_piece(p):
        return (owners + 2 * p, 2, steps + 1 + p)

    pl.semaphore_wait(barrier, owners + groups - 2)
    for way in (0, 1):
        key_hop(0, way).start()
    for half_ in (0, 1):
        for way in (0, 1):
            hop(0, way, half_).start()
    key_share(0, 0).start()

    in_piece = lax.broadcasted_iota(jnp.int32, (BASE, width), 0).astype(jnp.float32)
    first = lax.broadcasted_iota(jnp.int32, (BASE, width), 1) == 0

    def with_mark(values, k, offset):
        empty = first & (in_piece + offset >= count[k : k + 1, :])
        return jnp.where(empty, DEAD, values).astype(jnp.bfloat16)

    for t in range(owners // group_of):
        values = packed(pick(base_slot, group_of * BASE, ORDER[t] * group_of * BASE))
        for c in range(group_of):
            n = t * group_of + c
            piece = with_mark(values[c * BASE : (c + 1) * BASE, :], ORDER[t] * group_of + c, 0.0)
            if n == 0:
                own[owners] = piece
            else:
                outgoing[n] = piece
        if t == 0:
            lax.fori_loop(1, LEAD, start_dispatch, 0)
    values = packed(pick(side_slot, 2 * BASE))
    own[0] = with_mark(values[:BASE, :], 0, float(BASE))
    side[...] = with_mark(values[BASE:, :], 1, float(BASE))
    to_side().start()
    acc[...] = jnp.full_like(acc, -4.0)
    for s in range(1, steps + 1):
        if room(s) < POOL:
            for way in ways(s):
                for core in (0, 1):
                    pool[s, way, core, room(s) :] = jnp.zeros((POOL - room(s), width), jnp.bfloat16)

    def forward_both(piece):
        forward(*piece, 0).start()
        forward(*piece, 1).start()

    def base_arrives(p, carry):
        def one(k, inner):
            dispatch(k).wait_recv()
            return inner

        lax.fori_loop(2 * p, 2 * p + 2, one, 0)
        forward_both(base_piece(p))
        return carry

    def block(which, found, jb, ib, diagonal=False):
        right = found[pl.ds(jb * per_block, per_block)].reshape(per_block * BASE, width)
        left = own[pl.ds(ib * per_block, per_block)].reshape(per_block * BASE, width)
        scores = lax.dot_general(right, left, (((1,), (1,)), ((), ())), preferred_element_type=jnp.float32)
        drop = right[:, :128].astype(jnp.float32)[:, 0:1] > 1.5
        size = per_block * BASE
        if diagonal:
            drop = drop | (
                (jb == ib)
                & (
                    lax.broadcasted_iota(jnp.int32, (size, size), 0)
                    == lax.broadcasted_iota(jnp.int32, (size, size), 1)
                )
            )
        scores = jnp.where(drop, -1.0, scores)
        best = jnp.max(scores.reshape(size // 8, 8, size), axis=0)
        acc[which, ib] = jnp.maximum(acc[which, ib], best)

    def run(combos, kind, stride_j, start_j, stride_i, start_i):
        across = 2 if stride_i == 2 else blocks

        def body(x, carry):
            jb = stride_j * (x // across) + start_j
            ib = stride_i * (x % across) + start_i
            if kind == "own":
                block(0, own, jb, ib, diagonal=True)
            else:
                block(1, after, jb, ib)
                block(2, before, jb, ib)
            return carry

        lax.fori_loop(0, combos, body, 0)

    wide = lax.broadcasted_iota(jnp.int32, (1, 4 * POOL), 1)
    tall = lax.broadcasted_iota(jnp.int32, (4 * BASE, 1), 0)
    narrow = lax.broadcasted_iota(jnp.int32, (1, 128), 1)

    def select(s):
        parts = []
        for way in ways(s):
            zero, one = keys[s, way, 0], keys[s, way, 1]
            if way == 0:
                parts.append(jnp.where(narrow < POOL, zero, pltpu.roll(one, POOL, 1)))
            else:
                parts.append(jnp.where(narrow < POOL, pltpu.roll(zero, POOL, 1), one))
        n = len(parts)
        held = jnp.concatenate(parts, axis=1)
        lanes, outs = wide[:, : 2 * n * POOL], tall[: 2 * n * BASE, :]
        wanted = (((s - 1) * 2 + (outs // BASE) % 2) * BASE + outs % BASE + 1).astype(jnp.float32)
        match = (lanes // POOL == outs // BASE) & (held == wanted)
        chosen = jnp.where(match, 1.0, 0.0)
        there = pool[s, 0:n].reshape(2 * n * POOL, width)
        values_ = jnp.dot(chosen.astype(jnp.bfloat16), there, preferred_element_type=jnp.float32)
        none = jnp.sum(chosen, axis=1, keepdims=True) < 0.5
        front = lax.broadcasted_iota(jnp.int32, values_.shape, 1) == 0
        values_ = jnp.where(front & none, DEAD, values_).astype(jnp.bfloat16)
        begin, size, _ = tail_piece(s)
        own[begin : begin + size] = values_.reshape(size, BASE, width)

    to_side().wait_recv()
    forward_both(tail_piece(0))
    for s in range(1, steps + 1):
        for half_ in (0, 1):
            for way in ways(s):
                hop(s - 1, way, half_).wait_recv()
                if s < steps - way:
                    hop(s, way, half_).start()
        for way in ways(s):
            key_hop(s - 1, way).wait_recv()
            if s < steps - way:
                key_hop(s, way).start()
            key_share(s, way).start()
            share(s, way).start()
        if s < steps:
            per_step = (owners - LEAD + steps - 2) // (steps - 1)
            low = min(LEAD + per_step * (s - 1), owners)
            lax.fori_loop(low, min(low + per_step, owners), start_dispatch, 0)
        for way in ways(s):
            share(s, way).wait_recv()
            key_share(s, way).wait_recv()
        select(s)
        forward_both(tail_piece(s))
        if s == 2:
            dispatch(1).wait_recv()
            forward_both(base_piece(0))
        if s > 2:
            lax.fori_loop(2 * s - 5, 2 * s - 3, base_arrives, 0)
        if s == steps - 2:
            run(4, "own", 2, 0, 2, 0)
    key_share(0, 0).wait_recv()

    worst = jnp.maximum(key_out[...], keys[0, 0, 1])
    for s in range(1, steps + 1):
        for way in ways(s):
            worst = jnp.maximum(worst, jnp.maximum(keys[s, way, 0], keys[s, way, 1]))
    full[0] = worst

    def tell(d):
        return remote(
            full.at[0], full.at[d], full_send.at[d], full_recv.at[d], {"group": (group + d) % groups}
        )

    def start_tell(d, carry):
        tell(d).start()
        return carry

    lax.fori_loop(1, groups, start_tell, 0)

    def pair_arrives(pieces):
        for piece in pieces:
            forward(*piece, 0).wait_recv()
            forward(*piece, 1).wait_recv()

    def base_pair_arrives(p, carry):
        pair_arrives([base_piece(p)])
        return carry

    half = steps // 2
    done = 2 * steps - 3
    lax.fori_loop(done, owners // 2, base_arrives, 0)
    pair_arrives([tail_piece(s) for s in range(half + 1)])
    lax.fori_loop(0, half * 2, base_pair_arrives, 0)
    run(4, "pair", 2, 0, 2, 0)
    run(8, "own", 2, 1, 1, 0)
    run(4, "own", 2, 0, 2, 1)
    run(4, "pair", 2, 0, 2, 1)
    pair_arrives([tail_piece(s) for s in range(half + 1, steps + 1)])
    run(4, "pair", 0, 1, 1, 0)
    lax.fori_loop(half * 2, owners // 2, base_pair_arrives, 0)
    run(4, "pair", 0, 3, 1, 0)

    tiles = []
    for which in range(3):
        parts = []
        for b in range(blocks):
            best = jnp.max(acc[which, b], axis=0, keepdims=True)
            parts += [best[:, h * 128 : (h + 1) * 128] for h in range(per_block * BASE // 128)]
        early = jnp.concatenate([parts[len(parts) // 2 + ORDER.index(t)] for t in range(len(ORDER))], axis=0)
        late = jnp.concatenate(parts[: len(parts) // 2], axis=0)
        tiles += [early, late]
    spot = lax.broadcasted_iota(jnp.int32, tiles[0].shape, 1) // BASE
    per_tile = 128 // BASE
    for j in range(per_tile):
        mixed = tiles[0] if j == 0 else pltpu.roll(tiles[0], (-BASE * j) % 128, 1)
        for u in range(1, 6):
            moved = tiles[u] if u == j else pltpu.roll(tiles[u], (BASE * (u - j)) % 128, 1)
            mixed = jnp.where(spot >= u, moved, mixed)
        for t in range(owners // per_tile):
            k = per_tile * t + j
            if k == 0:
                got[k] = mixed[t : t + 1, :]
            else:
                ret[k] = mixed[t : t + 1, :]

    def give_back(k):
        return remote(ret.at[k], got.at[k], ret_send.at[k], ret_recv.at[k], {"dev": source(k)})

    def start_back(k, carry):
        give_back(owners - k).start()
        return carry

    lax.fori_loop(1, owners, start_back, 0)

    def drain(k, carry):
        dispatch(k).wait_send()
        return carry

    lax.fori_loop(1, owners, drain, 0)
    to_side().wait_send()
    key_share(0, 0).wait_send()
    for s in range(steps + 1):
        for way in (0, 1):
            if s < steps - way:
                hop(s, way, 0).wait_send()
                hop(s, way, 1).wait_send()
                key_hop(s, way).wait_send()
        if s > 0:
            for way in ways(s):
                share(s, way).wait_send()
                key_share(s, way).wait_send()
        forward(*tail_piece(s), 0).wait_send()
        forward(*tail_piece(s), 1).wait_send()

    def drain_pair(p, carry):
        forward(*base_piece(p), 0).wait_send()
        forward(*base_piece(p), 1).wait_send()
        return carry

    lax.fori_loop(0, owners // 2, drain_pair, 0)

    def wait_tell(d, carry):
        tell(d).wait()
        return carry

    lax.fori_loop(1, groups, wait_tell, 0)
    flag_ref[0, 0] = jnp.max(full[...])

    def wait_back(k, carry):
        give_back(k).wait()
        return carry

    lax.fori_loop(1, owners, wait_back, 0)

    table = got[...].reshape(owners, 128)
    high = table.astype(jnp.bfloat16)
    rest = table - high.astype(jnp.float32)
    middle = rest.astype(jnp.bfloat16)
    low_part = (rest - middle.astype(jnp.float32)).astype(jnp.bfloat16)
    stacked = jnp.concatenate([high, middle, low_part], axis=0)
    picks = jnp.concatenate([hot_b, hot_b, hot_b], axis=0)
    found = lax.dot_general(stacked, picks, (((0,), (0,)), ((), ())), preferred_element_type=jnp.float32)
    mine = lax.broadcasted_iota(jnp.int32, (CAP, 1), 0) == rank
    for which in range(3):
        kept = jnp.where(mine, found[which * CAP : (which + 1) * CAP, :], 0.0)
        line = jnp.sum(kept, axis=0, keepdims=True)
        for a in range(rows // 128):
            out_ref[which, a : a + 1, :] = line[:, a * 128 : (a + 1) * 128]


def all_slots(embeddings, owner):
    owners = lax.axis_size("dev")
    groups = lax.axis_size("group")
    rows, width = embeddings.shape
    vmem = pl.BlockSpec(memory_space=pltpu.VMEM)
    slots = (owners, CAP, width)
    hbm = pl.BlockSpec(memory_space=pltpu.HBM)
    return pl.pallas_call(
        functools.partial(padded, groups=groups, owners=owners),
        out_shape=jax.ShapeDtypeStruct((3, rows // 128, 128), jnp.float32),
        in_specs=[hbm, hbm],
        out_specs=vmem,
        scratch_shapes=[
            pltpu.VMEM((rows, width), jnp.float32),
            pltpu.VMEM((rows // 128, 128), jnp.int32),
            pltpu.VMEM((rows, width), jnp.bfloat16),
            pltpu.VMEM(slots, jnp.bfloat16),
            pltpu.VMEM(slots, jnp.bfloat16),
            pltpu.VMEM(slots, jnp.bfloat16),
            pltpu.VMEM(slots, jnp.bfloat16),
            pltpu.VMEM((3, owners // STAGE, 8, STAGE * CAP), jnp.float32),
            pltpu.VMEM((owners, 1, 128), jnp.float32),
            pltpu.VMEM((owners, 1, 128), jnp.float32),
            pltpu.SemaphoreType.DMA((2,)),
            pltpu.SemaphoreType.DMA((owners,)),
            pltpu.SemaphoreType.DMA((owners,)),
            pltpu.SemaphoreType.DMA((2, owners // PIECE)),
            pltpu.SemaphoreType.DMA((2, owners // PIECE)),
            pltpu.SemaphoreType.DMA((owners,)),
            pltpu.SemaphoreType.DMA((owners,)),
        ],
        compiler_params=pltpu.CompilerParams(
            collective_id=1, has_side_effects=True, vmem_limit_bytes=60 * 1024 * 1024
        ),
    )(embeddings, owner)


def few_slots(embeddings, owner):
    owners = lax.axis_size("dev")
    groups = lax.axis_size("group")
    rows, width = embeddings.shape
    steps = owners // 4
    vmem = pl.BlockSpec(memory_space=pltpu.VMEM)
    hbm = pl.BlockSpec(memory_space=pltpu.HBM)
    entries = (2 * owners, BASE, width)
    size = STAGE * CAP
    pieces = steps + 1 + owners // 2
    ring = pltpu.SemaphoreType.DMA((steps + 1, 2))
    halves = pltpu.SemaphoreType.DMA((steps + 1, 2, 2))
    return pl.pallas_call(
        functools.partial(pooled, groups=groups, owners=owners),
        out_shape=(
            jax.ShapeDtypeStruct((3, rows // 128, 128), jnp.float32),
            jax.ShapeDtypeStruct((1, 1), jnp.float32),
        ),
        in_specs=[hbm, hbm],
        out_specs=(vmem, pl.BlockSpec(memory_space=pltpu.SMEM)),
        scratch_shapes=[
            pltpu.VMEM((rows, width), jnp.float32),
            pltpu.VMEM((rows // 128, 128), jnp.int32),
            pltpu.VMEM((rows, width), jnp.bfloat16),
            pltpu.VMEM((owners, BASE, width), jnp.bfloat16),
            pltpu.VMEM((BASE, width), jnp.bfloat16),
            pltpu.VMEM(entries, jnp.bfloat16),
            pltpu.VMEM(entries, jnp.bfloat16),
            pltpu.VMEM(entries, jnp.bfloat16),
            pltpu.VMEM((3, 2 * owners * BASE // size, 8, size), jnp.float32),
            pltpu.VMEM((owners, 1, 128), jnp.float32),
            pltpu.VMEM((owners, 1, 128), jnp.float32),
            pltpu.VMEM((2, POOL, width), jnp.bfloat16),
            pltpu.VMEM((steps + 1, 2, 2, POOL, width), jnp.bfloat16),
            pltpu.VMEM((1, 128), jnp.float32),
            pltpu.VMEM((steps + 1, 2, 2, 1, 128), jnp.float32),
            pltpu.VMEM((groups, 1, 128), jnp.float32),
            pltpu.SemaphoreType.DMA((2,)),
            pltpu.SemaphoreType.DMA((owners,)),
            pltpu.SemaphoreType.DMA((owners,)),
            pltpu.SemaphoreType.DMA((2, pieces)),
            pltpu.SemaphoreType.DMA((2, pieces)),
            pltpu.SemaphoreType.DMA((owners,)),
            pltpu.SemaphoreType.DMA((owners,)),
            halves,
            halves,
            ring,
            ring,
            ring,
            ring,
            ring,
            ring,
            pltpu.SemaphoreType.DMA((groups,)),
            pltpu.SemaphoreType.DMA((groups,)),
            pltpu.SemaphoreType.DMA,
            pltpu.SemaphoreType.DMA,
        ],
        compiler_params=pltpu.CompilerParams(
            collective_id=0, has_side_effects=True, vmem_limit_bytes=60 * 1024 * 1024
        ),
    )(embeddings, owner)


def local(embeddings, owner):
    rows = embeddings.shape[0]
    lines = owner.reshape(rows // 128, 128)
    out, flag = few_slots(embeddings, lines)
    out = lax.cond(flag[0, 0] > FULL / 2, lambda e, o, kept: all_slots(e, o), lambda e, o, kept: kept, embeddings, lines, out)
    return tuple(out[which].reshape(rows) for which in range(3))


def solution(mesh):
    placed = (P(("group", "dev"), None), P(("group", "dev")))
    return jax.shard_map(
        local,
        mesh=mesh,
        in_specs=placed,
        out_specs=(P(("group", "dev")), P(("group", "dev")), P(("group", "dev"))),
        check_vma=False,
    )
```
